512 devices in a mesh: lon: 64 (over x_lo, z, core), lat: 8 (over y, x_hi).
Axes of the slice: x: 4 (x_hi: 2, x_lo: 2; x = x_hi * 2 + x_lo), y: 4, z: 16, core: 2. Of those that a mesh axis runs over, the one named last changes fastest.
Arguments:
- state_in: bfloat16 [8, 48, 147456], P(None, 'lat', 'lon'), may hold values from -60 to 60
- cotangent: bfloat16 [8, 48, 147456], P(None, 'lat', 'lon'), may hold values from -6 to 6
- w_qkv: bfloat16 [192, 576], replicated, may hold values from -0.4375 to 0.4375
- w_proj: bfloat16 [192, 192], replicated, may hold values from -0.4375 to 0.4375
- w_up: bfloat16 [192, 768], replicated, may hold values from -0.4375 to 0.4375
- w_down: bfloat16 [768, 192], replicated, may hold values from -0.21875 to 0.21875
- bias_table: float32 [32, 19872], P('lat'), may hold values from -4 to 300
- pad_valid: int32 [768], P('lon'), may hold values from 0 to 1, as said below
Outputs:
- grad_input: bfloat16 [8, 48, 147456], P(None, 'lat', 'lon')
- grad_qkv: float32 [192, 576], replicated
- grad_proj: float32 [192, 192], replicated
- grad_up: float32 [192, 768], replicated
- grad_down: float32 [768, 192], replicated
- grad_table: float32 [32, 19872], P('lat')
The draws below stay inside these ranges and needn't reach their ends.
Inputs may be any that keep to these rules, and one draw needn't show every extreme that they name: `pad_valid`: exactly 168 columns are 0, and they form one contiguous run around the longitude loop.
All inputs are finite; a program needn't handle non-finite values.
Results may differ from the reference program's by a relative error of at most 0.017.
Values may be sent and summed in bfloat16 or wider, within the bound.
A program may use at most 64 MiB of HBM per device.

```python
import jax
import jax.numpy as jnp
from jax import lax

C = 192
HEADS = 6
MLP = 768
WZ = 2
WH = 6
WW = 12
POS = 3312
Z = 8
NLAT = 48
NLON = 768
TYPES = 32
PADW = 168
TOKENS = 294912


def draw_state_in(key, part):
    key = jax.random.fold_in(key, 11)
    scale_key, main_key = jax.random.split(key, 2)
    channel_scale = jnp.exp(jax.random.uniform(scale_key, (C,), jnp.float32) * 2.302585)
    values = jax.random.normal(main_key, (Z, NLAT, NLON, C), jnp.float32) * channel_scale / 3.0
    values = jnp.clip(values, -60.0, 60.0)
    return values.reshape(Z, NLAT, NLON * C).astype(jnp.bfloat16)


def draw_bias_table(key, part):
    key = jax.random.fold_in(key, 23)
    base_key = jax.random.fold_in(key, 0)
    pair_count = HEADS * POS // 2
    baseline = jnp.clip(jax.random.normal(base_key, (TYPES, pair_count, 2), jnp.float32), -4.0, 4.0)
    return baseline.reshape(TYPES, HEADS * POS)


def draw_pad_valid(key, part):
    key = jax.random.fold_in(key, 41)
    run_start = jax.random.randint(key, (), 0, NLON)
    distance = (jnp.arange(NLON) - run_start) % NLON
    return (distance >= PADW).astype(jnp.int32)


def steps_of(stream_key, extent, shards, smallest, largest):
    factor_of, own = 1.0, jax.random.fold_in(stream_key, 6)
    for position, blocks in shards:
        draws = jnp.exp(jax.random.uniform(jax.random.fold_in(own, position), (blocks,), jnp.float32, smallest / len(shards), largest / len(shards)))
        factor_of = factor_of * jnp.repeat(draws, extent[position] // blocks).reshape([-1 if axis == position else 1 for axis in range(len(extent))])
    return factor_of


def bell_draw(key, extent, deviation, reach, shards=(), dtype=jnp.bfloat16):
    factor_of = steps_of(key, extent, shards, -0.22, 0.18) if shards else 1.0
    array = jax.random.normal(key, extent, jnp.float32) * deviation * factor_of
    return jnp.minimum(jnp.maximum(array, -reach), reach).astype(dtype)


def setup_inputs(seed: int = 0) -> dict:
    streams_of = jax.random.split(jax.random.key(seed), 9)
    return {
        "state_in": draw_state_in(jax.random.fold_in(streams_of[8], 71), 0),
        "cotangent": bell_draw(streams_of[1], (Z, NLAT, NLON * C), 1.0, 6.0, ((1, 8), (2, 64))),
        "w_qkv": bell_draw(streams_of[2], (C, 3 * C), C ** -0.5, 0.4375),
        "w_proj": bell_draw(streams_of[3], (C, C), C ** -0.5, 0.4375),
        "w_up": bell_draw(streams_of[4], (C, MLP), C ** -0.5, 0.4375),
        "w_down": bell_draw(streams_of[5], (MLP, C), MLP ** -0.5, 0.21875),
        "bias_table": draw_bias_table(jax.random.fold_in(streams_of[8], 71), 0),
        "pad_valid": draw_pad_valid(jax.random.fold_in(streams_of[8], 71), 0),
    }


MASKED_SCORE = -1e+30
NORM_EPS = 1e-05

def layer_norm(inputs):
    average = lax.optimization_barrier(jnp.mean(inputs, axis=-1, keepdims=True))
    centred = inputs - average
    inv_std = lax.rsqrt(lax.optimization_barrier(jnp.mean(centred * centred, axis=-1, keepdims=True)) + NORM_EPS)
    return (centred * inv_std, inv_std)

def norm_back(upstream, normed, inv_std):
    return inv_std * (upstream - lax.optimization_barrier(jnp.mean(upstream, axis=-1, keepdims=True)) - normed * lax.optimization_barrier(jnp.mean(upstream * normed, axis=-1, keepdims=True)))

def gelu_exact(inputs):
    return 0.5 * inputs * (1.0 + lax.erf(inputs * 0.7071067811865476))

def gelu_slope(inputs):
    return 0.5 * (1.0 + lax.erf(inputs * 0.7071067811865476)) + inputs * jnp.exp(-0.5 * inputs * inputs) * 0.3989422804014327

def flat_dot(left_op, right_op):
    flat = left_op.reshape(-1, left_op.shape[-1])
    product = jnp.dot(flat, right_op, preferred_element_type=jnp.float32)
    return product.reshape(left_op.shape[:-1] + (right_op.shape[-1],))

def grad_dot(left_op, right_op):
    return jnp.dot(left_op.reshape(-1, left_op.shape[-1]).T, right_op.reshape(-1, right_op.shape[-1]), preferred_element_type=jnp.float32)

def batched(formula, left_op, right_op):
    return jnp.einsum(formula, left_op.astype(jnp.float32), right_op.astype(jnp.float32))

def spread_table():
    span = 2 * WW - 1
    row_level = jnp.arange(WZ)[:, None, None, None, None, None, None]
    row_lat = jnp.arange(WH)[None, :, None, None, None, None, None]
    row_off = jnp.arange(span)[None, None, :, None, None, None, None]
    col_query = jnp.arange(WW)[None, None, None, :, None, None, None]
    col_level = jnp.arange(WZ)[None, None, None, None, :, None, None]
    col_lat = jnp.arange(WH)[None, None, None, None, None, :, None]
    col_key = jnp.arange(WW)[None, None, None, None, None, None, :]
    hit = (row_level == col_level) & (row_lat == col_lat) & (row_off == col_query - col_key + WW - 1)
    return hit.astype(jnp.float32).reshape(WZ * WH * span, WW * WZ * WH * WW)

def window_bias(bias_rows):
    window_count = bias_rows.shape[0]
    span = 2 * WW - 1
    grid = bias_rows.reshape(window_count, HEADS, WZ, WZ, WH, WH, span).transpose(0, 1, 2, 4, 3, 5, 6)
    grid = grid.reshape(window_count * HEADS * WZ * WH, WZ * WH * span)
    spread = jnp.dot(grid, spread_table(), precision=lax.Precision.HIGHEST)
    window_cells = WZ * WH * WW
    return spread.reshape(window_count, HEADS, window_cells, window_cells)

def bias_grad(dscore):
    window_count = dscore.shape[0]
    span = 2 * WW - 1
    flat = dscore.reshape(window_count * HEADS * WZ * WH, WW * WZ * WH * WW)
    grid = jnp.dot(flat, spread_table().T, precision=lax.Precision.HIGHEST)
    grid = grid.reshape(window_count, HEADS, WZ, WH, WZ, WH, span).transpose(0, 1, 2, 4, 3, 5, 6)
    return grid.reshape(window_count, HEADS * WZ * WZ * WH * WH * span)

def to_windows(field_in):
    z_windows = field_in.shape[0] // WZ
    h_windows = field_in.shape[1] // WH
    w_windows = field_in.shape[2] // WW
    feature_count = field_in.shape[3]
    blocked = field_in.reshape(z_windows, WZ, h_windows, WH, w_windows, WW, feature_count).transpose(0, 2, 4, 1, 3, 5, 6)
    return blocked.reshape(z_windows * h_windows * w_windows, WZ * WH * WW, feature_count)

def from_windows(blocks, level_cells, row_cells, col_cells):
    feature_count = blocks.shape[-1]
    blocked = blocks.reshape(level_cells // WZ, row_cells // WH, col_cells // WW, WZ, WH, WW, feature_count).transpose(0, 3, 1, 4, 2, 5, 6)
    return blocked.reshape(level_cells, row_cells, col_cells, feature_count)

def attend(activation, labels, bias_rows, w_qkv):
    window_count, window_cells, channels = activation.shape
    head_dim = channels // HEADS
    qkv_rows = flat_dot(activation, w_qkv).astype(jnp.bfloat16).reshape(window_count, window_cells, 3, HEADS, head_dim)
    queries = qkv_rows[:, :, 0]
    key_rows = qkv_rows[:, :, 1]
    values = qkv_rows[:, :, 2]
    scores = batched('nqhd,nkhd->nhqk', queries, key_rows) * head_dim ** (-0.5) + window_bias(bias_rows)
    allowed = labels[:, None, :, None] == labels[:, None, None, :]
    scores = jnp.where(allowed, scores, MASKED_SCORE)
    peak_val = lax.optimization_barrier(jnp.max(scores, axis=-1, keepdims=True))
    raised = jnp.exp(scores - peak_val)
    attn_prob = raised / lax.optimization_barrier(jnp.sum(raised, axis=-1, keepdims=True))
    prob_b = attn_prob.astype(jnp.bfloat16)
    mixed = batched('nhqk,nkhd->nqhd', prob_b, values).astype(jnp.bfloat16).reshape(window_count, window_cells, channels)
    return (mixed, (queries, key_rows, values, attn_prob, prob_b))

def attend_back(dmixed, saved, w_qkv):
    queries, key_rows, values, attn_prob, prob_b = saved
    window_count, window_cells, heads_here, head_dim = queries.shape
    dmixed = dmixed.reshape(window_count, window_cells, heads_here, head_dim)
    prob_grad = batched('nqhd,nkhd->nhqk', dmixed, values)
    value_grad = batched('nhqk,nqhd->nkhd', prob_b, dmixed)
    dscore = attn_prob * (prob_grad - lax.optimization_barrier(jnp.sum(attn_prob * prob_grad, axis=-1, keepdims=True)))
    row_grads = bias_grad(dscore)
    dscore_b = dscore.astype(jnp.bfloat16)
    scale_now = head_dim ** (-0.5)
    query_grad = batched('nhqk,nkhd->nqhd', dscore_b, key_rows) * scale_now
    key_grad = batched('nhqk,nqhd->nkhd', dscore_b, queries) * scale_now
    qkv_grads = jnp.stack([query_grad, key_grad, value_grad], axis=2).astype(jnp.bfloat16)
    qkv_grads = qkv_grads.reshape(window_count, window_cells, 3 * heads_here * head_dim)
    act_grads = flat_dot(qkv_grads, w_qkv.T)
    return (qkv_grads, act_grads, row_grads)

def middle(wide_in, mixed, gmask, w_proj, w_up, w_down):
    state_mid = (wide_in + flat_dot(mixed, w_proj)).astype(jnp.bfloat16)
    normed, inv_std = layer_norm(state_mid.astype(jnp.float32))
    normed_b = normed.astype(jnp.bfloat16)
    pre_act = flat_dot(normed_b, w_up)
    hidden = gelu_exact(pre_act).astype(jnp.bfloat16)
    down_part = grad_dot(hidden, gmask)
    hidden_grad = flat_dot(gmask, w_down.T)
    pre_grad = (hidden_grad * gelu_slope(pre_act)).astype(jnp.bfloat16)
    up_part = grad_dot(normed_b, pre_grad)
    normed_grad = flat_dot(pre_grad, w_up.T)
    dstate = (gmask.astype(jnp.float32) + norm_back(normed_grad, normed, inv_std)).astype(jnp.bfloat16)
    proj_part = grad_dot(mixed, dstate)
    dmixed = flat_dot(dstate, w_proj.T).astype(jnp.bfloat16)
    return (dstate, dmixed, proj_part, up_part, down_part)

def reference(state_in, cotangent, w_qkv, w_proj, w_up, w_down, bias_table, pad_valid):
    shifts = (-(WZ // 2), -(WH // 2), -(WW // 2))
    cells_in = jnp.roll(state_in.reshape(Z, NLAT, NLON, C), shifts, axis=(0, 1, 2))
    grad_cells = jnp.roll(cotangent.reshape(Z, NLAT, NLON, C), shifts, axis=(0, 1, 2))
    valid_cols = jnp.roll(pad_valid, shifts[2])
    level_tag = (jnp.arange(Z) >= Z - WZ // 2).astype(jnp.int32)
    row_tag = (jnp.arange(NLAT) >= NLAT - WH // 2).astype(jnp.int32)
    labels = level_tag[:, None, None] * 4 + row_tag[None, :, None] * 2 + valid_cols[None, None, :]
    gmask = grad_cells * valid_cols[None, None, :, None].astype(jnp.bfloat16)
    window_cells = WZ * WH * WW
    group_size = NLON // WW
    group_count = Z // WZ * (NLAT // WH)
    group_types = (jnp.arange(NLAT // WH)[None, :] * (Z // WZ) + jnp.arange(Z // WZ)[:, None]).astype(jnp.int32)
    type_grid = jnp.broadcast_to(group_types.reshape(group_count, 1), (group_count, group_size)).astype(jnp.int32)
    scan_inputs = (to_windows(cells_in).reshape(group_count, group_size, window_cells, C), to_windows(gmask).reshape(group_count, group_size, window_cells, C), to_windows(labels[..., None])[..., 0].reshape(group_count, group_size, window_cells), type_grid)

    def window_group(running, scan_item):
        sum_qkv, sum_proj, sum_up, sum_down, sum_table = running
        group_in, group_grad, group_label, group_ids = scan_item
        wide_in = group_in.astype(jnp.float32)
        normed, inv_std = layer_norm(wide_in)
        activation = normed.astype(jnp.bfloat16)
        mixed, saved = attend(activation, group_label, jnp.take(bias_table, group_ids, axis=0), w_qkv)
        dstate, dmixed, proj_part, up_part, down_part = middle(wide_in, mixed, group_grad, w_proj, w_up, w_down)
        qkv_grads, act_grads, row_grads = attend_back(dmixed, saved, w_qkv)
        qkv_part = grad_dot(activation, qkv_grads)
        input_grad = (dstate.astype(jnp.float32) + norm_back(act_grads, normed, inv_std)).astype(jnp.bfloat16)
        one_hot = (group_ids[:, None] == jnp.arange(TYPES)[None, :]).astype(jnp.float32)
        sum_table = sum_table + jnp.dot(one_hot.T, row_grads, precision=lax.Precision.HIGHEST)
        return ((sum_qkv + qkv_part, sum_proj + proj_part, sum_up + up_part, sum_down + down_part, sum_table), input_grad)
    zeros_init = (jnp.zeros((C, 3 * C), jnp.float32), jnp.zeros((C, C), jnp.float32), jnp.zeros((C, MLP), jnp.float32), jnp.zeros((MLP, C), jnp.float32), jnp.zeros((TYPES, bias_table.shape[1]), jnp.float32))
    totals, input_grads = lax.scan(window_group, zeros_init, scan_inputs)
    grad_shifted = from_windows(input_grads.reshape(-1, window_cells, C), Z, NLAT, NLON)
    grad_input = jnp.roll(grad_shifted, (WZ // 2, WH // 2, WW // 2), axis=(0, 1, 2)).reshape(Z, NLAT, NLON * C)
    factor = float(TOKENS) ** (-0.5)
    return (grad_input, totals[0] * factor, totals[1] * factor, totals[2] * factor, totals[3] * factor, totals[4])
```

```python
import functools

import jax
import jax.numpy as jnp
import numpy as np
from jax import lax
from jax.experimental import pallas as pl
from jax.experimental.pallas import tpu as pltpu
from jax.sharding import PartitionSpec as P

F32 = jnp.float32
BF16 = jnp.bfloat16
MESH = pl.DeviceIdType.MESH

C = 192
HEADS = 6
HEAD_DIM = 32
MLP = 768
WZ = 2
WH = 6
WW = 12
LEVELS = 8
WIN = WZ * WH * WW
NWIN = LEVELS // WZ
CELLS = WIN * NWIN
CH = WW // 2
RH = WH // 2
SLAB = LEVELS * RH
QUARTER = CH * SLAB
PACK = 2 * C
EXTRA = 16
SPAN = 2 * WW - 1
ZR = WZ * WH
TROWS = NWIN * HEADS * ZR
TCOLS = ZR * SPAN
TSEG = WH * SPAN
WCOLS = 3 * C + C + 2 * MLP
WTILES = (C // 16) * (WCOLS // 128)
TLANES = -(-TCOLS // 128)
TTILES = (TROWS // 16) * TLANES
XL = 2
NORM_EPS = 1e-5
MASKED = -1e30
VMEM_LIMIT = 56 * 1024 * 1024


def up_to(value, unit):
    return -(-value // unit) * unit


class Plan:
    def __init__(self, lon, lat):
        self.lon, self.lat = lon, lat
        self.nz = lon // (2 * XL)
        self.plane = XL * lat
        self.wt = -(-WTILES // (2 * self.plane))
        self.tt = -(-TTILES // (2 * XL))
        self.wrows = self.wt * 16 // self.nz
        self.trows = self.tt * 16 // self.nz
        self.toff = up_to(self.wrows, 8)
        self.zrows = up_to(self.toff + self.trows, 16)
        assert self.wrows * self.nz == self.wt * 16
        assert self.trows * self.nz == self.tt * 16


def cell_order():
    perm = np.zeros((CELLS, CELLS), np.float32)
    for w in range(NWIN):
        for c in range(WW):
            for z in range(WZ):
                for r in range(WH):
                    row = w * WIN + c * ZR + z * WH + r
                    quarter = (r // RH) * 2 + c // CH
                    col = quarter * QUARTER + (c % CH) * SLAB + w * WZ * RH + z * RH + r % RH
                    perm[row, col] = 1
    return perm


def slab_order():
    perm = np.zeros((2 * SLAB, LEVELS * 8), np.float32)
    for rs in range(2):
        for w in range(NWIN):
            for z in range(WZ):
                for r in range(RH):
                    row = rs * SLAB + w * WZ * RH + z * RH + r
                    perm[row, ((2 * w + z + WZ // 2) % LEVELS) * 8 + rs * RH + r] = 1
    return perm


def table_rows():
    perm = np.zeros((TROWS, TROWS), np.float32)
    for t in range(NWIN):
        for s in range(HEADS * ZR):
            perm[t * HEADS * ZR + s, s * NWIN + t] = 1
    return perm


def table_lanes():
    perm = np.zeros((TCOLS, TCOLS), np.float32)
    for b in range(ZR):
        for d in range(SPAN):
            perm[b * SPAN + d, (SPAN - 1 - d) * ZR + b] = 1
    return perm


def table_sums():
    hit = np.zeros((WW, WIN, TCOLS), np.float32)
    for ci in range(WW):
        for cj in range(WW):
            for b in range(ZR):
                hit[ci, cj * ZR + b, b * SPAN + ci - cj + WW - 1] = 1
    return hit


def column_of_cell():
    hit = np.zeros((WIN, EXTRA), np.float32)
    for c in range(WW):
        hit[c * ZR : (c + 1) * ZR, c] = 1
    return hit


def dot(a, b):
    return lax.dot_general(a, b, (((1,), (0,)), ((), ())), preferred_element_type=F32)


def dot_nt(a, b):
    return lax.dot_general(a, b, (((1,), (1,)), ((), ())), preferred_element_type=F32)


def dot_tn(a, b):
    return lax.dot_general(a, b, (((0,), (0,)), ((), ())), preferred_element_type=F32)


def neighbours(plan):
    lon, lat = lax.axis_index("lon"), lax.axis_index("lat")
    lon_b, lon_a = lax.rem(lon + plan.lon - 1, plan.lon), lax.rem(lon + 1, plan.lon)
    lat_b, lat_a = lax.rem(lat + plan.lat - 1, plan.lat), lax.rem(lat + 1, plan.lat)
    before = [(lon_b, lat), (lon, lat_b), (lon_b, lat_b)]
    after = [(lon_a, lat), (lon, lat_a), (lon_a, lat_a)]
    return before, after


def remote(src, dst, send, recv, place):
    return pltpu.make_async_remote_copy(
        src_ref=src, dst_ref=dst, send_sem=send, recv_sem=recv,
        device_id={"lon": place[0], "lat": place[1]}, device_id_type=MESH,
    )


def greet(place):
    pl.semaphore_signal(
        pltpu.get_barrier_semaphore(), inc=1,
        device_id={"lon": place[0], "lat": place[1]}, device_id_type=MESH,
    )


def enter_kernel(plan, x_ref, g_ref, valid_ref, slab_ref, out_ref, home, packed, send, recv, ssem, rsem):
    before, after = neighbours(plan)
    for place in before + after:
        greet(place)
    slab = slab_ref[...]
    packed[...] = jnp.zeros_like(packed)
    for part, ref in enumerate((x_ref, g_ref)):
        home[...] = jnp.zeros_like(home)
        for level in range(LEVELS):
            home[8 * level : 8 * level + WH, :] = ref[level].astype(F32)
        rows = dot(slab, home[...].astype(BF16))
        for c in range(WW):
            for rs in range(2):
                piece = rows[rs * SLAB : (rs + 1) * SLAB, c * C : (c + 1) * C]
                if part == 1:
                    piece = piece * valid_ref[0, c].astype(F32)
                packed[
                    rs * 2 + c // CH, (c % CH) * SLAB : (c % CH + 1) * SLAB, part * C : (part + 1) * C
                ] = piece
    for c in range(WW):
        mark = jnp.full((1, PACK), valid_ref[0, c].astype(F32), F32)
        for rs in range(2):
            packed[rs * 2 + c // CH, QUARTER + c % CH : QUARTER + c % CH + 1, :] = mark
    send[...] = packed[...].astype(BF16)
    pl.semaphore_wait(pltpu.get_barrier_semaphore(), 6)
    copies = [
        remote(send.at[2], recv.at[1], ssem.at[0], rsem.at[0], before[0]),
        remote(send.at[1], recv.at[2], ssem.at[1], rsem.at[1], before[1]),
        remote(send.at[0], recv.at[3], ssem.at[2], rsem.at[2], before[2]),
    ]
    for copy in copies:
        copy.start()
    out_ref[0] = send[3]
    for copy in copies:
        copy.wait()
    for q in range(1, 4):
        out_ref[q] = recv[q]


def enter_frame(plan, state, cotangent, valid):
    shape = (4, QUARTER + EXTRA, PACK)
    vmem = pl.BlockSpec(memory_space=pltpu.VMEM)
    return pl.pallas_call(
        functools.partial(enter_kernel, plan),
        out_shape=jax.ShapeDtypeStruct(shape, BF16),
        in_specs=[vmem, vmem, pl.BlockSpec(memory_space=pltpu.SMEM), vmem],
        out_specs=vmem,
        scratch_shapes=[
            pltpu.VMEM((LEVELS * 8, WW * C), F32),
            pltpu.VMEM(shape, F32),
            pltpu.VMEM(shape, BF16),
            pltpu.VMEM(shape, BF16),
            pltpu.SemaphoreType.DMA((3,)),
            pltpu.SemaphoreType.DMA((3,)),
        ],
        compiler_params=pltpu.CompilerParams(
            collective_id=0, has_side_effects=True, vmem_limit_bytes=VMEM_LIMIT
        ),
        name="enter_frame",
    )(state, cotangent, valid.reshape(1, WW), jnp.asarray(slab_order(), BF16))


def normed_of(v):
    centred = v - jnp.mean(v, axis=-1, keepdims=True)
    inv = lax.rsqrt(jnp.mean(centred * centred, axis=-1, keepdims=True) + NORM_EPS)
    return centred * inv, inv


def norm_back(up, normed, inv):
    return inv * (
        up
        - jnp.mean(up, axis=-1, keepdims=True)
        - normed * jnp.mean(up * normed, axis=-1, keepdims=True)
    )


def block_kernel(
    plan,
    frame_ref, w_qkv, w_proj, w_up, w_down, table_ref,
    order_ref, back_ref, trow_ref, tlane_ref, tsum_ref, ccol_ref,
    dx_ref, wout_ref, tout_ref,
    xs, gm, act, act_inv, q_s, k_s, v_s, o_s, dh_s, dout_s, b_s, m_s, du_s, dqkv_s,
    tn, bias, prob, dcol, total, tgrad,
):
    hm = []
    lane = lax.broadcasted_iota(jnp.int32, (1, C), 1)
    for h in range(HEADS):
        hm.append(jnp.where(lane // HEAD_DIM == h, 1.0, 0.0).astype(BF16))
    scale = HEAD_DIM ** (-0.5)

    quarters = frame_ref[:, :QUARTER, :].reshape(CELLS, PACK)
    cells = dot(order_ref[...], quarters)
    xs[...] = cells[:, :C]
    gm[...] = cells[:, C:].astype(BF16)

    for h in range(HEADS):
        for zi in range(WZ):
            for zj in range(WZ):
                for ri in range(WH):
                    seg = ((h * WZ + zi) * WZ + zj) * WH + ri
                    row = (h * ZR + zi * WH + ri) * NWIN
                    tn[row : row + NWIN, zj * TSEG : (zj + 1) * TSEG] = table_ref[
                        :, seg * TSEG : (seg + 1) * TSEG
                    ]
    left = tn[...]
    spread = jnp.zeros((TROWS, TCOLS), F32)
    for _ in range(3):
        term = left.astype(BF16)
        left = left - term.astype(F32)
        spread += dot(dot(trow_ref[...], term).astype(BF16), tlane_ref[...])
    tn[...] = spread

    marks = jnp.concatenate(
        [
            frame_ref[0, QUARTER : QUARTER + EXTRA, :WIN][:CH].astype(F32),
            frame_ref[1, QUARTER : QUARTER + EXTRA, :WIN][:CH].astype(F32),
            jnp.zeros((EXTRA - WW, WIN), F32),
        ],
        axis=0,
    ).astype(BF16)
    ccol = ccol_ref[...]
    same = dot(ccol, marks) == lax.dot_general(
        marks, ccol, (((0,), (1,)), ((), ())), preferred_element_type=F32
    )
    ii = lax.broadcasted_iota(jnp.int32, (WIN, WIN), 0)
    jj = lax.broadcasted_iota(jnp.int32, (WIN, WIN), 1)
    low_i, low_j = (lax.rem(ii, WH) >= RH).astype(jnp.int32), (lax.rem(jj, WH) >= RH).astype(jnp.int32)
    seam = lax.axis_index("lat") == plan.lat - 1
    open_rows = jnp.where(seam, 0, 1)
    same = same & ((low_i == low_j) | (open_rows == 1))
    top_i, top_j = lax.rem(ii // WH, WZ), lax.rem(jj // WH, WZ)
    barred = jnp.where(same, 0.0, MASKED)
    barred_top = jnp.where(top_i == top_j, barred, MASKED)

    for t in range(NWIN):
        bar = barred_top if t == NWIN - 1 else barred
        for ci in range(WW):
            rows = tn[t * HEADS * ZR : (t + 1) * HEADS * ZR, (WW - 1 - ci) * ZR : (WW - 1 - ci) * ZR + WIN]
            for h in range(HEADS):
                bias[t * HEADS + h, ci * ZR : (ci + 1) * ZR, :] = (
                    rows[h * ZR : (h + 1) * ZR, :] + bar[ci * ZR : (ci + 1) * ZR, :]
                )

    normed, inv = normed_of(xs[...])
    a = normed.astype(BF16)
    act[...] = a
    q_s[...] = dot(a, w_qkv[:, :C]).astype(BF16)
    k_s[...] = dot(a, w_qkv[:, C : 2 * C]).astype(BF16)
    v_s[...] = dot(a, w_qkv[:, 2 * C :]).astype(BF16)

    def forward(w, carry):
        at = pl.ds(pl.multiple_of(w * WIN, WIN), WIN)
        q, k, v = q_s[at, :], k_s[at, :], v_s[at, :]
        mixed = jnp.zeros((WIN, C), F32)
        for h in range(HEADS):
            s = dot_nt(q * hm[h], k) * scale + bias[w * HEADS + h]
            e = jnp.exp(s - jnp.max(s, axis=-1, keepdims=True))
            p = e * (1.0 / jnp.sum(e, axis=-1, keepdims=True))
            prob[w * HEADS + h] = p
            mixed += dot(p.astype(BF16), v * hm[h])
        o_s[at, :] = mixed.astype(BF16)
        return carry

    lax.fori_loop(0, NWIN, forward, 0)

    def middle(w, carry):
        at = pl.ds(pl.multiple_of(w * WIN, WIN), WIN)
        hs = (xs[at, :] + dot(o_s[at, :], w_proj[...])).astype(BF16).astype(F32)
        n2, inv2 = normed_of(hs)
        b = n2.astype(BF16)
        b_s[at, :] = b
        u = dot(b, w_up[...])
        cdf = 0.5 * (1.0 + lax.erf(u * 0.7071067811865476))
        m_s[at, :] = (u * cdf).astype(BF16)
        slope = cdf + u * jnp.exp(-0.5 * u * u) * 0.3989422804014327
        g = gm[at, :]
        du = (dot_nt(g, w_down[...]) * slope).astype(BF16)
        du_s[at, :] = du
        dh = (g.astype(F32) + norm_back(dot_nt(du, w_up[...]), n2, inv2)).astype(BF16)
        dh_s[at, :] = dh
        dout_s[at, :] = dot_nt(dh, w_proj[...]).astype(BF16)
        return carry

    lax.fori_loop(0, NWIN, middle, 0)
    total[:, 3 * C : 4 * C] = dot_tn(o_s[...], dh_s[...])
    total[:, 4 * C : 4 * C + MLP] = dot_tn(b_s[...], du_s[...])
    total[:, 4 * C + MLP :] = dot_tn(gm[...], m_s[...])

    for w in range(NWIN):
        at = pl.ds(w * WIN, WIN)
        q, k, v, do = q_s[at, :], k_s[at, :], v_s[at, :], dout_s[at, :]
        dq, dk, dv = (jnp.zeros((WIN, C), F32) for _ in range(3))
        for h in range(HEADS):
            p = prob[w * HEADS + h]
            do_h = do * hm[h]
            dp = dot_nt(do_h, v)
            ds = p * (dp - jnp.sum(p * dp, axis=-1, keepdims=True))
            first = (w * HEADS + h) * ZR
            for ci in range(WW):
                dcol[ci, first : first + ZR, :] = ds[ci * ZR : (ci + 1) * ZR, :]
            dsb = ds.astype(BF16)
            dq += dot(dsb, k * hm[h])
            dk += dot_tn(dsb, q * hm[h])
            dv += dot_tn(p.astype(BF16), do_h)
        dqkv_s[at, 0:C] = (dq * scale).astype(BF16)
        dqkv_s[at, C : 2 * C] = (dk * scale).astype(BF16)
        dqkv_s[at, 2 * C :] = dv.astype(BF16)

    dqkv = dqkv_s[...]
    total[:, : 3 * C] = dot_tn(act[...], dqkv)
    back = dot_nt(dqkv, w_qkv[...])
    normed, inv = normed_of(xs[...])
    dxs = (dh_s[...].astype(F32) + norm_back(back, normed, inv)).astype(BF16)
    dx_ref[...] = dot(back_ref[...], dxs).astype(BF16).reshape(4, QUARTER, C)

    grad = jnp.zeros((TROWS, TCOLS), F32)
    for ci in range(WW):
        grad += dot(dcol[ci].astype(BF16), tsum_ref[ci])
    tgrad[...] = jnp.zeros_like(tgrad)
    tgrad[:, :TCOLS] = dot_tn(trow_ref[...], grad.astype(BF16))
    tiles = TROWS // 16 * TLANES
    for i in range(4 * plan.tt):
        core, rest = divmod(i, XL * plan.tt)
        place = (core, rest // plan.tt, rest % plan.tt)
        if i < tiles:
            r, l = divmod(i, TLANES)
            tout_ref[place] = tgrad[r * 16 : r * 16 + 16, l * 128 : l * 128 + 128].astype(BF16)
        else:
            tout_ref[place] = jnp.zeros((16, 128), BF16)
    for i in range(2 * plan.plane * plan.wt):
        core, rest = divmod(i, plan.plane * plan.wt)
        place = (core, rest // plan.wt, rest % plan.wt)
        if i < WTILES:
            r, l = divmod(i, WCOLS // 128)
            wout_ref[place] = total[r * 16 : r * 16 + 16, l * 128 : l * 128 + 128].astype(BF16)
        else:
            wout_ref[place] = jnp.zeros((16, 128), BF16)


def block(plan, frame, w_qkv, w_proj, w_up, w_down, table):
    vmem = pl.BlockSpec(memory_space=pltpu.VMEM)
    order = cell_order()
    return pl.pallas_call(
        functools.partial(block_kernel, plan),
        out_shape=(
            jax.ShapeDtypeStruct((4, QUARTER, C), BF16),
            jax.ShapeDtypeStruct((2, plan.plane, plan.wt, 16, 128), BF16),
            jax.ShapeDtypeStruct((2, XL, plan.tt, 16, 128), BF16),
        ),
        in_specs=[vmem] * 12,
        out_specs=(vmem, vmem, vmem),
        scratch_shapes=[
            pltpu.VMEM((CELLS, C), F32),
            pltpu.VMEM((CELLS, C), BF16),
            pltpu.VMEM((CELLS, C), BF16),
            pltpu.VMEM((CELLS, 1), F32),
            pltpu.VMEM((CELLS, C), BF16),
            pltpu.VMEM((CELLS, C), BF16),
            pltpu.VMEM((CELLS, C), BF16),
            pltpu.VMEM((CELLS, C), BF16),
            pltpu.VMEM((CELLS, C), BF16),
            pltpu.VMEM((CELLS, C), BF16),
            pltpu.VMEM((CELLS, C), BF16),
            pltpu.VMEM((CELLS, MLP), BF16),
            pltpu.VMEM((CELLS, MLP), BF16),
            pltpu.VMEM((CELLS, 3 * C), BF16),
            pltpu.VMEM((TROWS, TCOLS), F32),
            pltpu.VMEM((NWIN * HEADS, WIN, WIN), F32),
            pltpu.VMEM((NWIN * HEADS, WIN, WIN), F32),
            pltpu.VMEM((WW, TROWS, WIN), F32),
            pltpu.VMEM((C, WCOLS), F32),
            pltpu.VMEM((TROWS, TLANES * 128), F32),
        ],
        compiler_params=pltpu.CompilerParams(vmem_limit_bytes=VMEM_LIMIT),
        name="block",
    )(
        frame, w_qkv, w_proj, w_up, w_down, table,
        jnp.asarray(order, BF16), jnp.asarray(order.T, BF16), jnp.asarray(table_rows(), BF16),
        jnp.asarray(table_lanes(), BF16), jnp.asarray(table_sums(), BF16),
        jnp.asarray(column_of_cell(), BF16),
    )


def share_kernel(
    plan, dx_ref, wsend, tsend, home_ref, wall_ref, tall_ref,
    hrecv, wr1, tr1, w1, t1, wr2, tr2, rows, zrows, zsend, zrecv, zall, wall, tall,
    hs, hr, c1s, c1r, p2s, p2r, t2s, t2r, z1s, z1r, z2s, z2r, p3s, p3r, t3s, t3r, c4s, c4r,
):
    lon, lat = lax.axis_index("lon"), lax.axis_index("lat")
    nz, plane = plan.nz, plan.plane
    core = lax.rem(lon, 2)
    z = lax.rem(lon // 2, nz)
    xl = lon // (2 * nz)
    me = xl * plan.lat + lat

    def at(p, zz, cc):
        return (p // plan.lat) * (2 * nz) + zz * 2 + cc, lax.rem(p, plan.lat)

    def plane_peer(d):
        return lax.rem(me + d, plane)

    def z_peer(d):
        return lax.rem(z + d, nz)

    def plane_from(d):
        return lax.rem(me - d + plane, plane)

    other = at(me, z, 1 - core)
    across = at((1 - xl) * plan.lat + lat, z, core)
    before, after = neighbours(plan)
    greet(other)
    for place in before + after:
        greet(place)

    def greet_plane(d, carry):
        greet(at(plane_peer(d), z, core))
        return carry

    def greet_z(d, carry):
        greet(at(me, z_peer(d), core))
        return carry

    lax.fori_loop(1, plane, greet_plane, 0)
    lax.fori_loop(1, nz, greet_z, 0)
    pl.semaphore_wait(pltpu.get_barrier_semaphore(), 7 + plane - 1 + nz - 1)

    first = [
        remote(wsend.at[1 - core], wr1, c1s.at[0], c1r.at[0], other),
        remote(tsend.at[1 - core], tr1, c1s.at[1], c1r.at[1], other),
    ]
    for copy in first:
        copy.start()
    home = [
        remote(dx_ref.at[1], hrecv.at[2], hs.at[0], hr.at[0], after[0]),
        remote(dx_ref.at[2], hrecv.at[1], hs.at[1], hr.at[1], after[1]),
        remote(dx_ref.at[3], hrecv.at[0], hs.at[2], hr.at[2], after[2]),
    ]
    for copy in home:
        copy.start()
    home_ref[3] = dx_ref[0]
    for copy in first:
        copy.wait_recv()

    def piece_out(d):
        p = plane_peer(d)
        return remote(w1.at[p], wr2.at[d], p2s.at[d], p2r.at[d], at(p, z, core))

    def send_piece(d, carry):
        p = plane_peer(d)
        w1[p] = (wsend[core, p].astype(F32) + wr1[p].astype(F32)).astype(BF16)
        piece_out(d).start()
        return carry

    lax.fori_loop(1, plane, send_piece, 0)
    t1[...] = (tsend[core, 1 - xl].astype(F32) + tr1[1 - xl].astype(F32)).astype(BF16)
    table_out = remote(t1, tr2, t2s.at[0], t2r.at[0], across)
    table_out.start()
    wsum = wsend[core, me].astype(F32) + wr1[me].astype(F32)
    tsum = tsend[core, xl].astype(F32) + tr1[xl].astype(F32)

    def take_piece(d, acc):
        piece_out(d).wait_recv()
        return acc + wr2[d].astype(F32)

    wsum = lax.fori_loop(1, plane, take_piece, wsum)
    table_out.wait_recv()
    tsum = tsum + tr2[...].astype(F32)

    wlen, tlen = plan.wt * 16, plan.tt * 16
    rows[:wlen, :] = wsum.reshape(wlen, 128)
    rows[wlen:, :] = tsum.reshape(tlen, 128)
    zrows[...] = jnp.zeros_like(zrows)
    wr, tr, to = plan.wrows, plan.trows, plan.toff
    for i in range(nz):
        zrows[i, :wr, :] = rows[i * wr : (i + 1) * wr, :]
        zrows[i, to : to + tr, :] = rows[wlen + i * tr : wlen + (i + 1) * tr, :]
    zsend[...] = zrows[...].astype(BF16)

    def z_out(d):
        p = z_peer(d)
        return remote(zsend.at[p], zrecv.at[d], z1s.at[d], z1r.at[d], at(me, p, core))

    def z_back(d):
        return remote(zall.at[z], zall.at[z], z2s.at[d], z2r.at[d], at(me, z_peer(d), core))

    def start_z_out(d, carry):
        z_out(d).start()
        return carry

    def take_z(d, acc):
        z_out(d).wait_recv()
        return acc + zrecv[d].astype(F32)

    def start_z_back(d, carry):
        z_back(d).start()
        return carry

    def wait_z_back(d, carry):
        z_back(d).wait_recv()
        return carry

    lax.fori_loop(1, nz, start_z_out, 0)
    zall[z] = lax.fori_loop(1, nz, take_z, zsend[z].astype(F32)).astype(BF16)
    lax.fori_loop(1, nz, start_z_back, 0)
    lax.fori_loop(1, nz, wait_z_back, 0)
    zrows[...] = zall[...].astype(F32)
    for i in range(nz):
        rows[i * wr : (i + 1) * wr, :] = zrows[i, :wr, :]
        rows[wlen + i * tr : wlen + (i + 1) * tr, :] = zrows[i, to : to + tr, :]
    wall[core, me] = rows[:wlen, :].astype(BF16).reshape(plan.wt, 16, 128)
    tall[core, xl] = rows[wlen:, :].astype(BF16).reshape(plan.tt, 16, 128)

    def sum_out(d):
        mine = wall.at[core, me]
        return remote(mine, mine, p3s.at[d], p3r.at[d], at(plane_peer(d), z, core))

    def hand_over(d):
        held = wall.at[core, plane_from(d)]
        return remote(held, held, c4s.at[d], c4r.at[d], other)

    def table_hand(i, owner):
        held = tall.at[core, owner]
        return remote(held, held, c4s.at[plane + i], c4r.at[plane + i], other)

    def start_sum_out(d, carry):
        sum_out(d).start()
        return carry

    def forward_sum(d, carry):
        sum_out(d).wait_recv()
        hand_over(d).start()
        return carry

    mine_t = tall.at[core, xl]
    table_back = remote(mine_t, mine_t, t3s.at[0], t3r.at[0], across)
    table_back.start()
    lax.fori_loop(1, plane, start_sum_out, 0)
    hand_over(0).start()
    table_hand(0, xl).start()
    table_back.wait_recv()
    table_hand(1, 1 - xl).start()
    lax.fori_loop(1, plane, forward_sum, 0)

    def wait_hand(d, carry):
        hand_over(d).wait_recv()
        return carry

    lax.fori_loop(0, plane, wait_hand, 0)
    table_hand(0, xl).wait_recv()
    table_hand(1, 1 - xl).wait_recv()
    for copy in home:
        copy.wait_recv()
    for q in range(3):
        home_ref[q] = hrecv[q]
    wall_ref[...] = wall[...]
    tall_ref[...] = tall[...]

    for copy in first + home + [table_out, table_back, table_hand(0, xl), table_hand(1, 1 - xl)]:
        copy.wait_send()

    def drain_plane(d, carry):
        piece_out(d).wait_send()
        sum_out(d).wait_send()
        return carry

    def drain_z(d, carry):
        z_out(d).wait_send()
        z_back(d).wait_send()
        return carry

    def drain_hand(d, carry):
        hand_over(d).wait_send()
        return carry

    lax.fori_loop(1, plane, drain_plane, 0)
    lax.fori_loop(1, nz, drain_z, 0)
    lax.fori_loop(0, plane, drain_hand, 0)


def share(plan, dx, wsend, tsend):
    vmem = pl.BlockSpec(memory_space=pltpu.VMEM)
    plane, nz = plan.plane, plan.nz
    sem = pltpu.SemaphoreType.DMA
    lines = (plan.wt + plan.tt) * 16
    return pl.pallas_call(
        functools.partial(share_kernel, plan),
        out_shape=(
            jax.ShapeDtypeStruct(dx.shape, BF16),
            jax.ShapeDtypeStruct(wsend.shape, BF16),
            jax.ShapeDtypeStruct(tsend.shape, BF16),
        ),
        in_specs=[vmem] * 3,
        out_specs=(vmem,) * 3,
        scratch_shapes=[
            pltpu.VMEM((3, QUARTER, C), BF16),
            pltpu.VMEM(wsend.shape[1:], BF16),
            pltpu.VMEM(tsend.shape[1:], BF16),
            pltpu.VMEM(wsend.shape[1:], BF16),
            pltpu.VMEM(tsend.shape[2:], BF16),
            pltpu.VMEM(wsend.shape[1:], BF16),
            pltpu.VMEM(tsend.shape[2:], BF16),
            pltpu.VMEM((lines, 128), F32),
            pltpu.VMEM((nz, plan.zrows, 128), F32),
            pltpu.VMEM((nz, plan.zrows, 128), BF16),
            pltpu.VMEM((nz, plan.zrows, 128), BF16),
            pltpu.VMEM((nz, plan.zrows, 128), BF16),
            pltpu.VMEM(wsend.shape, BF16),
            pltpu.VMEM(tsend.shape, BF16),
            sem((3,)), sem((3,)), sem((2,)), sem((2,)), sem((plane,)), sem((plane,)),
            sem((1,)), sem((1,)), sem((nz,)), sem((nz,)), sem((nz,)), sem((nz,)),
            sem((plane,)), sem((plane,)), sem((1,)), sem((1,)), sem((plane + 2,)), sem((plane + 2,)),
        ],
        compiler_params=pltpu.CompilerParams(
            collective_id=1, has_side_effects=True, vmem_limit_bytes=VMEM_LIMIT
        ),
        name="share",
    )(dx, wsend, tsend)


def write_kernel(
    plan, factor, home_ref, wall, tall, slab_ref,
    dx_ref, qkv_ref, proj_ref, up_ref, down_ref, table_ref, band, total, tgrad,
):
    for c in range(WW):
        for rs in range(2):
            band[rs * SLAB : (rs + 1) * SLAB, c * C : (c + 1) * C] = home_ref[
                rs * 2 + c // CH, (c % CH) * SLAB : (c % CH + 1) * SLAB, :
            ].astype(F32)
    rows = dot_tn(slab_ref[...], band[...].astype(BF16))
    for level in range(LEVELS):
        dx_ref[level] = rows[8 * level : 8 * level + WH, :].astype(BF16)
    for i in range(WTILES):
        core, rest = divmod(i, plan.plane * plan.wt)
        r, l = divmod(i, WCOLS // 128)
        total[r * 16 : r * 16 + 16, l * 128 : l * 128 + 128] = (
            wall[core, rest // plan.wt, rest % plan.wt].astype(F32) * factor
        )
    qkv_ref[...] = total[:, : 3 * C]
    proj_ref[...] = total[:, 3 * C : 4 * C]
    up_ref[...] = total[:, 4 * C : 4 * C + MLP]
    down_ref[...] = total[:, 4 * C + MLP :].T
    for i in range(TTILES):
        core, rest = divmod(i, XL * plan.tt)
        r, l = divmod(i, TLANES)
        tgrad[r * 16 : r * 16 + 16, l * 128 : l * 128 + 128] = tall[
            core, rest // plan.tt, rest % plan.tt
        ].astype(F32)
    for h in range(HEADS):
        for zi in range(WZ):
            for zj in range(WZ):
                for ri in range(WH):
                    seg = ((h * WZ + zi) * WZ + zj) * WH + ri
                    row = (h * ZR + zi * WH + ri) * NWIN
                    table_ref[:, seg * TSEG : (seg + 1) * TSEG] = tgrad[
                        row : row + NWIN, zj * TSEG : (zj + 1) * TSEG
                    ]


def write(plan, home, wall, tall):
    vmem = pl.BlockSpec(memory_space=pltpu.VMEM)
    factor = float(CELLS * plan.lon * plan.lat) ** (-0.5)
    return pl.pallas_call(
        functools.partial(write_kernel, plan, factor),
        out_shape=(
            jax.ShapeDtypeStruct((LEVELS, WH, WW * C), BF16),
            jax.ShapeDtypeStruct((C, 3 * C), F32),
            jax.ShapeDtypeStruct((C, C), F32),
            jax.ShapeDtypeStruct((C, MLP), F32),
            jax.ShapeDtypeStruct((MLP, C), F32),
            jax.ShapeDtypeStruct((NWIN, HEADS * ZR * ZR * SPAN), F32),
        ),
        in_specs=[vmem] * 4,
        out_specs=(vmem,) * 6,
        scratch_shapes=[
            pltpu.VMEM((2 * SLAB, WW * C), F32),
            pltpu.VMEM((C, WCOLS), F32),
            pltpu.VMEM((TROWS, TLANES * 128), F32),
        ],
        compiler_params=pltpu.CompilerParams(vmem_limit_bytes=VMEM_LIMIT),
        name="write",
    )(home, wall, tall, jnp.asarray(slab_order(), BF16))


def per_device(plan, state_in, cotangent, w_qkv, w_proj, w_up, w_down, bias_table, pad_valid):
    frame = enter_frame(plan, state_in, cotangent, pad_valid)
    dx, wsend, tsend = block(plan, frame, w_qkv, w_proj, w_up, w_down, bias_table)
    return write(plan, *share(plan, dx, wsend, tsend))


def solution(mesh):
    plan = Plan(mesh.shape["lon"], mesh.shape["lat"])
    return jax.shard_map(
        functools.partial(per_device, plan),
        mesh=mesh,
        in_specs=(
            P(None, "lat", "lon"),
            P(None, "lat", "lon"),
            P(),
            P(),
            P(),
            P(),
            P("lat", None),
            P("lon"),
        ),
        out_specs=(P(None, "lat", "lon"), P(), P(), P(), P(), P("lat", None)),
        check_vma=False,
    )
```

```python
import functools

import jax
import jax.numpy as jnp
import numpy as np
from jax import lax
from jax.experimental import pallas as pl
from jax.experimental.pallas import tpu as pltpu
from jax.sharding import PartitionSpec as P

F32 = jnp.float32
BF16 = jnp.bfloat16
MESH = pl.DeviceIdType.MESH

C = 192
HEADS = 6
HEAD_DIM = 32
MLP = 768
WZ = 2
WH = 6
WW = 12
LEVELS = 8
WIN = WZ * WH * WW
NWIN = LEVELS // WZ
CELLS = WIN * NWIN
CH = WW // 2
RH = WH // 2
SLAB = LEVELS * RH
QUARTER = CH * SLAB
PACK = 2 * C
EXTRA = 16
SPAN = 2 * WW - 1
ZR = WZ * WH
PAIRS = WW // 2
STRIP = 2 * ZR
TROWS = NWIN * HEADS * ZR
TCOLS = ZR * SPAN
TSEG = WH * SPAN
ECOLS = 1792
LCOLS = 640
KCOLS = (SPAN + 1) * ZR
TLANES = -(-TCOLS // 128)
TTILES = (TROWS // 16) * TLANES
XL = 2
NORM_EPS = 1e-5
MASKED = -1e30
VMEM_LIMIT = 56 * 1024 * 1024


def up_to(value, unit):
    return -(-value // unit) * unit


class Plan:
    def __init__(self, lon, lat):
        self.lon, self.lat = lon, lat
        self.nz = lon // (2 * XL)
        self.plane = XL * lat
        self.tt = -(-TTILES // (2 * XL))
        self.trows = self.tt * 16 // self.nz
        assert self.trows * self.nz == self.tt * 16

    def weight_tiles(self, columns):
        tiles = -(-(C // 16) * (columns // 128) // (2 * self.plane))
        while tiles * 16 % self.nz:
            tiles += 1
        return tiles


def cell_order():
    perm = np.zeros((CELLS, CELLS), np.float32)
    for w in range(NWIN):
        for c in range(WW):
            for z in range(WZ):
                for r in range(WH):
                    row = w * WIN + c * ZR + z * WH + r
                    quarter = (r // RH) * 2 + c // CH
                    col = quarter * QUARTER + (c % CH) * SLAB + w * WZ * RH + z * RH + r % RH
                    perm[row, col] = 1
    return perm


def slab_order():
    perm = np.zeros((2 * SLAB, LEVELS * WH), np.float32)
    for rs in range(2):
        for w in range(NWIN):
            for z in range(WZ):
                for r in range(RH):
                    row = rs * SLAB + w * WZ * RH + z * RH + r
                    perm[row, (rs * RH + r) * LEVELS + (2 * w + z + WZ // 2) % LEVELS] = 1
    return perm


def table_rows(odd):
    perm = np.zeros((2 * TROWS, TROWS), np.float32)
    for t in range(NWIN):
        for h in range(HEADS):
            for b in range(ZR):
                perm[((t * HEADS + h) * 2 + odd) * ZR + b, (h * ZR + b) * NWIN + t] = 1
    return perm


def table_lanes(odd):
    perm = np.zeros((TCOLS, KCOLS), np.float32)
    for b in range(ZR):
        for d in range(SPAN):
            perm[b * SPAN + d, (SPAN - 1 - d + odd) * ZR + b] = 1
    return perm


def table_sums():
    hit = np.zeros((PAIRS, WIN, KCOLS), np.float32)
    for pair in range(PAIRS):
        for cj in range(WW):
            for b in range(ZR):
                hit[pair, cj * ZR + b, (cj - 2 * pair + WW - 1) * ZR + b] = 1
    return hit


def column_of_cell():
    hit = np.zeros((WIN, EXTRA), np.float32)
    for c in range(WW):
        hit[c * ZR : (c + 1) * ZR, c] = 1
    return hit


def dot(a, b):
    return lax.dot_general(a, b, (((1,), (0,)), ((), ())), preferred_element_type=F32)


def dot_nt(a, b):
    return lax.dot_general(a, b, (((1,), (1,)), ((), ())), preferred_element_type=F32)


def dot_tn(a, b):
    return lax.dot_general(a, b, (((0,), (0,)), ((), ())), preferred_element_type=F32)


def neighbours(plan):
    lon, lat = lax.axis_index("lon"), lax.axis_index("lat")
    lon_b, lon_a = lax.rem(lon + plan.lon - 1, plan.lon), lax.rem(lon + 1, plan.lon)
    lat_b, lat_a = lax.rem(lat + plan.lat - 1, plan.lat), lax.rem(lat + 1, plan.lat)
    before = [(lon_b, lat), (lon, lat_b), (lon_b, lat_b)]
    after = [(lon_a, lat), (lon, lat_a), (lon_a, lat_a)]
    return before, after


def remote(src, dst, send, recv, place):
    return pltpu.make_async_remote_copy(
        src_ref=src, dst_ref=dst, send_sem=send, recv_sem=recv,
        device_id={"lon": place[0], "lat": place[1]}, device_id_type=MESH,
    )


def greet(place):
    pl.semaphore_signal(
        pltpu.get_barrier_semaphore(), inc=1,
        device_id={"lon": place[0], "lat": place[1]}, device_id_type=MESH,
    )


def each(first, last, act):
    def step(i, carry):
        act(i)
        return carry

    lax.fori_loop(first, last, step, 0)


class Spot:
    def __init__(self, plan):
        self.plan = plan
        self.lon, self.lat = lax.axis_index("lon"), lax.axis_index("lat")
        self.nz, self.plane = plan.nz, plan.plane
        self.core = lax.rem(self.lon, 2)
        self.z = lax.rem(self.lon // 2, self.nz)
        self.xl = self.lon // (2 * self.nz)
        self.me = self.xl * plan.lat + self.lat
        self.other = self.at(self.me, self.z, 1 - self.core)
        self.across = self.at((1 - self.xl) * plan.lat + self.lat, self.z, self.core)

    def at(self, p, z, core):
        return (p // self.plan.lat) * (2 * self.nz) + z * 2 + core, lax.rem(p, self.plan.lat)

    def plane_peer(self, d):
        return lax.rem(self.me + d, self.plane)

    def plane_from(self, d):
        return lax.rem(self.me - d + self.plane, self.plane)

    def z_peer(self, d):
        return lax.rem(self.z + d, self.nz)

    def greet_all(self):
        greet(self.other)
        each(1, self.plane, lambda d: greet(self.at(self.plane_peer(d), self.z, self.core)))
        each(1, self.nz, lambda d: greet(self.at(self.me, self.z_peer(d), self.core)))
        return 1 + self.plane - 1 + self.nz - 1


class Sum:
    def __init__(self, plan, columns, table):
        self.plan, self.table = plan, table
        self.columns = columns
        self.wt = plan.weight_tiles(columns)
        self.tt = plan.tt if table else 0
        self.wr = self.wt * 16 // plan.nz
        self.tr = plan.trows if table else 0
        self.zr = up_to(self.wr + self.tr, 16)

    def out_shapes(self):
        plan = self.plan
        shapes = [jax.ShapeDtypeStruct((2, plan.plane, self.wt, 16, 128), BF16)]
        if self.table:
            shapes.append(jax.ShapeDtypeStruct((2, XL, self.tt, 16, 128), BF16))
        return shapes

    def scratch(self):
        plan, wt, tt = self.plan, self.wt, self.tt
        plane, nz = plan.plane, plan.nz
        sem = pltpu.SemaphoreType.DMA
        shapes = dict(
            wsend=pltpu.VMEM((2, plane, wt, 16, 128), BF16),
            wr1=pltpu.VMEM((plane, wt, 16, 128), BF16),
            w1=pltpu.VMEM((plane, wt, 16, 128), BF16),
            wr2=pltpu.VMEM((plane, wt, 16, 128), BF16),
            wall=pltpu.VMEM((2, plane, wt, 16, 128), BF16),
            rows=pltpu.VMEM(((wt + tt) * 16, 128), F32),
            zrows=pltpu.VMEM((nz, self.zr, 128), F32),
            zsend=pltpu.VMEM((nz, self.zr, 128), BF16),
            zrecv=pltpu.VMEM((nz, self.zr, 128), BF16),
            zall=pltpu.VMEM((nz, self.zr, 128), BF16),
            c1s=sem((2,)), c1r=sem((2,)), p2s=sem((plane,)), p2r=sem((plane,)),
            z1s=sem((nz,)), z1r=sem((nz,)), z2s=sem((nz,)), z2r=sem((nz,)),
            p3s=sem((plane,)), p3r=sem((plane,)), c4s=sem((plane + 2,)), c4r=sem((plane + 2,)),
        )
        if self.table:
            shapes.update(
                tsend=pltpu.VMEM((2, XL, tt, 16, 128), BF16),
                tr1=pltpu.VMEM((XL, tt, 16, 128), BF16),
                t1=pltpu.VMEM((tt, 16, 128), BF16),
                tr2=pltpu.VMEM((tt, 16, 128), BF16),
                tall=pltpu.VMEM((2, XL, tt, 16, 128), BF16),
                t2s=sem((1,)), t2r=sem((1,)), t3s=sem((1,)), t3r=sem((1,)),
            )
        self.names = list(shapes)
        return list(shapes.values())

    def bind(self, spot, refs):
        self.spot = spot
        for name, ref in zip(self.names, refs):
            setattr(self, name, ref)

    def core_copies(self):
        s = self.spot
        copies = [remote(self.wsend.at[1 - s.core], self.wr1, self.c1s.at[0], self.c1r.at[0], s.other)]
        if self.table:
            copies.append(remote(self.tsend.at[1 - s.core], self.tr1, self.c1s.at[1], self.c1r.at[1], s.other))
        return copies

    def piece(self, d):
        s = self.spot
        p = s.plane_peer(d)
        return remote(self.w1.at[p], self.wr2.at[d], self.p2s.at[d], self.p2r.at[d], s.at(p, s.z, s.core))

    def table_piece(self):
        return remote(self.t1, self.tr2, self.t2s.at[0], self.t2r.at[0], self.spot.across)

    def z_out(self, d):
        s = self.spot
        p = s.z_peer(d)
        return remote(self.zsend.at[p], self.zrecv.at[d], self.z1s.at[d], self.z1r.at[d], s.at(s.me, p, s.core))

    def z_home(self, d):
        s = self.spot
        mine = self.zall.at[s.z]
        return remote(mine, mine, self.z2s.at[d], self.z2r.at[d], s.at(s.me, s.z_peer(d), s.core))

    def spread(self, d):
        s = self.spot
        mine = self.wall.at[s.core, s.me]
        return remote(mine, mine, self.p3s.at[d], self.p3r.at[d], s.at(s.plane_peer(d), s.z, s.core))

    def table_spread(self):
        s = self.spot
        mine = self.tall.at[s.core, s.xl]
        return remote(mine, mine, self.t3s.at[0], self.t3r.at[0], s.across)

    def hand(self, d):
        s = self.spot
        held = self.wall.at[s.core, s.plane_from(d)]
        return remote(held, held, self.c4s.at[d], self.c4r.at[d], s.other)

    def table_hand(self, i):
        s = self.spot
        held = self.tall.at[s.core, s.xl if i == 0 else 1 - s.xl]
        n = self.plan.plane + i
        return remote(held, held, self.c4s.at[n], self.c4r.at[n], s.other)

    def fill(self, total, table=None):
        plan = self.plan
        jobs = [(total, self.wsend, self.columns // 128, C // 16, plan.plane, self.wt)]
        if self.table:
            jobs.append((table, self.tsend, TLANES, TROWS // 16, XL, self.tt))
        for ref, out, lanes, rows, parts, tiles in jobs:
            for i in range(2 * parts * tiles):
                core, rest = divmod(i, parts * tiles)
                place = (core, rest // tiles, rest % tiles)
                if i < rows * lanes:
                    r, l = divmod(i, lanes)
                    out[place] = ref[r * 16 : r * 16 + 16, l * 128 : l * 128 + 128].astype(BF16)
                else:
                    out[place] = jnp.zeros((16, 128), BF16)

    def core_start(self):
        for copy in self.core_copies():
            copy.start()

    def plane_start(self):
        s = self.spot
        for copy in self.core_copies():
            copy.wait_recv()

        def send(d):
            p = s.plane_peer(d)
            self.w1[p] = (self.wsend[s.core, p].astype(F32) + self.wr1[p].astype(F32)).astype(BF16)
            self.piece(d).start()

        if self.table:
            far = 1 - s.xl
            self.t1[...] = (self.tsend[s.core, far].astype(F32) + self.tr1[far].astype(F32)).astype(BF16)
            self.table_piece().start()
        each(1, s.plane, send)

    def z_start(self):
        s, plan = self.spot, self.plan
        wlen = self.wt * 16

        def take(d, acc):
            self.piece(d).wait_recv()
            return acc + self.wr2[d].astype(F32)

        first = self.wsend[s.core, s.me].astype(F32) + self.wr1[s.me].astype(F32)
        self.rows[:wlen, :] = lax.fori_loop(1, s.plane, take, first).reshape(wlen, 128)
        if self.table:
            self.table_piece().wait_recv()
            near = self.tsend[s.core, s.xl].astype(F32) + self.tr1[s.xl].astype(F32)
            self.rows[wlen:, :] = (near + self.tr2[...].astype(F32)).reshape(self.tt * 16, 128)
        wr, tr = self.wr, self.tr
        if wr + tr < self.zr:
            self.zrows[...] = jnp.zeros_like(self.zrows)
        for i in range(s.nz):
            self.zrows[i, :wr, :] = self.rows[i * wr : (i + 1) * wr, :]
            if tr:
                self.zrows[i, wr : wr + tr, :] = self.rows[wlen + i * tr : wlen + (i + 1) * tr, :]
        self.zsend[...] = self.zrows[...].astype(BF16)
        each(1, s.nz, lambda d: self.z_out(d).start())

    def z_back(self):
        s = self.spot

        def take(d, acc):
            self.z_out(d).wait_recv()
            return acc + self.zrecv[d].astype(F32)

        self.zall[s.z] = lax.fori_loop(1, s.nz, take, self.zsend[s.z].astype(F32)).astype(BF16)
        each(1, s.nz, lambda d: self.z_home(d).start())

    def plane_back(self):
        s, plan = self.spot, self.plan
        each(1, s.nz, lambda d: self.z_home(d).wait_recv())
        self.zrows[...] = self.zall[...].astype(F32)
        wr, tr, wlen = self.wr, self.tr, self.wt * 16
        for i in range(s.nz):
            self.rows[i * wr : (i + 1) * wr, :] = self.zrows[i, :wr, :]
            if tr:
                self.rows[wlen + i * tr : wlen + (i + 1) * tr, :] = self.zrows[i, wr : wr + tr, :]
        if self.table:
            self.tall[s.core, s.xl] = self.rows[wlen:, :].astype(BF16).reshape(self.tt, 16, 128)
            self.table_spread().start()
            self.table_hand(0).start()
        self.wall[s.core, s.me] = self.rows[:wlen, :].astype(BF16).reshape(self.wt, 16, 128)
        each(1, s.plane, lambda d: self.spread(d).start())
        self.hand(0).start()

    def hand_over(self):
        if self.table:
            self.table_spread().wait_recv()
            self.table_hand(1).start()

        def forward(d):
            self.spread(d).wait_recv()
            self.hand(d).start()

        each(1, self.spot.plane, forward)

    def finish(self):
        each(0, self.spot.plane, lambda d: self.hand(d).wait_recv())
        if self.table:
            self.table_hand(0).wait_recv()
            self.table_hand(1).wait_recv()

    def drain(self):
        s = self.spot
        for copy in self.core_copies():
            copy.wait_send()
        if self.table:
            for copy in (self.table_piece(), self.table_spread(), self.table_hand(0), self.table_hand(1)):
                copy.wait_send()

        def plane(d):
            self.piece(d).wait_send()
            self.spread(d).wait_send()

        def over_z(d):
            self.z_out(d).wait_send()
            self.z_home(d).wait_send()

        each(1, s.plane, plane)
        each(1, s.nz, over_z)
        each(0, s.plane, lambda d: self.hand(d).wait_send())


def normed_of(v):
    centred = v - jnp.mean(v, axis=-1, keepdims=True)
    inv = lax.rsqrt(jnp.mean(centred * centred, axis=-1, keepdims=True) + NORM_EPS)
    return centred * inv, inv


def norm_back(up, normed, inv):
    return inv * (
        up
        - jnp.mean(up, axis=-1, keepdims=True)
        - normed * jnp.mean(up * normed, axis=-1, keepdims=True)
    )


FAR = (
    "w_qkv", "w_proj", "w_up", "w_downt", "order", "back",
    "even_row", "odd_row", "even_lane", "odd_lane", "tsum", "ccol",
)
QUARTERS = (4, QUARTER + EXTRA, PACK)
SCRATCH = dict(
    packed=(QUARTERS, F32),
    outward=(QUARTERS, BF16),
    frame=(QUARTERS, BF16),
    tn=((TROWS, TCOLS), F32),
    spread=((2 * TROWS, KCOLS), F32),
    bars=((2, WIN, WIN), F32),
    xs=((CELLS, C), F32),
    gm=((CELLS, C), BF16),
    act=((CELLS, C), BF16),
    q=((CELLS, C), BF16),
    k=((CELLS, C), BF16),
    v=((CELLS, C), BF16),
    qkvt=((NWIN, 3 * C, WIN), BF16),
    ot=((NWIN, C, WIN), BF16),
    dot=((NWIN, C, WIN), BF16),
    dh=((CELLS, C), BF16),
    dout=((CELLS, C), BF16),
    b=((CELLS, C), BF16),
    m=((CELLS, MLP), BF16),
    du=((CELLS, MLP), BF16),
    dqkvt=((3 * C, WIN), BF16),
    back=((CELLS, C), F32),
    wqkvt=((3 * C, C), BF16),
    bias=((NWIN * HEADS, WIN, WIN), F32),
    prob=((NWIN * HEADS, WIN, WIN), F32),
    dcol=((PAIRS, 2 * TROWS, WIN), BF16),
    early=((C, ECOLS), F32),
    late=((C, LCOLS), F32),
    lsum=((3 * C, C), F32),
    tgrad=((TROWS, TLANES * 128), F32),
    send=((4, QUARTER, C), BF16),
    hrecv=((4, QUARTER, C), BF16),
)


def block_kernel(plan, sums, *refs):
    x_ref, g_ref, valid_ref, slab_ref, table_ref = refs[:5]
    far = refs[5 : 5 + len(FAR)]
    refs = refs[5 + len(FAR) :]
    home_ref, early_ref, late_ref, tall_ref = refs[:4]
    near = dict(zip(FAR, refs[4 : 4 + len(FAR)]))
    refs = refs[4 + len(FAR) :]
    s = dict(zip(SCRATCH, refs))
    refs = refs[len(SCRATCH) :]
    fs, es, er, hs, hr, outs = refs[:6]
    refs = refs[6:]
    spot = Spot(plan)
    early, late = sums
    early.bind(spot, refs[: len(early.names)])
    late.bind(spot, refs[len(early.names) :])
    before, after = neighbours(plan)
    for place in before + after:
        greet(place)
    greeted = spot.greet_all() + 6
    fetch = [pltpu.make_async_copy(src, near[name], fs.at[n]) for n, (name, src) in enumerate(zip(FAR, far))]
    for copy in fetch:
        copy.start()
    w_qkv, w_proj, w_up, w_downt, order_ref, back_ref, tsum_ref, ccol_ref = (
        near[n] for n in ("w_qkv", "w_proj", "w_up", "w_downt", "order", "back", "tsum", "ccol")
    )

    hm = []
    lane = lax.broadcasted_iota(jnp.int32, (1, C), 1)
    for h in range(HEADS):
        hm.append(jnp.where(lane // HEAD_DIM == h, 1.0, 0.0).astype(BF16))
    scale = HEAD_DIM ** (-0.5)

    slab = slab_ref[...]
    packed, outward, frame = s["packed"], s["outward"], s["frame"]
    packed[:, QUARTER:, :] = jnp.zeros((4, EXTRA, PACK), F32)
    for part, ref in enumerate((x_ref, g_ref)):
        rows = dot(slab, ref[...])
        for c in range(WW):
            for rs in range(2):
                piece = rows[rs * SLAB : (rs + 1) * SLAB, c * C : (c + 1) * C]
                if part == 1:
                    piece = piece * valid_ref[0, c].astype(F32)
                packed[
                    rs * 2 + c // CH, (c % CH) * SLAB : (c % CH + 1) * SLAB, part * C : (part + 1) * C
                ] = piece
    for c in range(WW):
        mark = jnp.full((1, PACK), valid_ref[0, c].astype(F32), F32)
        for rs in range(2):
            packed[rs * 2 + c // CH, QUARTER + c % CH : QUARTER + c % CH + 1, :] = mark
    outward[...] = packed[...].astype(BF16)
    for h in range(HEADS):
        for zi in range(WZ):
            for zj in range(WZ):
                for ri in range(WH):
                    seg = ((h * WZ + zi) * WZ + zj) * WH + ri
                    row = (h * ZR + zi * WH + ri) * NWIN
                    s["tn"][row : row + NWIN, zj * TSEG : (zj + 1) * TSEG] = table_ref[
                        :, seg * TSEG : (seg + 1) * TSEG
                    ]
    pl.semaphore_wait(pltpu.get_barrier_semaphore(), greeted)
    enter = [
        remote(outward.at[2], frame.at[1], es.at[0], er.at[0], before[0]),
        remote(outward.at[1], frame.at[2], es.at[1], er.at[1], before[1]),
        remote(outward.at[0], frame.at[3], es.at[2], er.at[2], before[2]),
    ]
    for copy in enter:
        copy.start()
    frame[0] = outward[3]

    for copy in fetch:
        copy.wait()
    left = s["tn"][...]
    for n in range(3):
        term = left.astype(BF16)
        left = left - term.astype(F32)
        part = dot(dot_tn(near["even_row"][...], term).astype(BF16), near["even_lane"][...]) + dot(
            dot_tn(near["odd_row"][...], term).astype(BF16), near["odd_lane"][...]
        )
        if n == 0:
            s["spread"][...] = part
        else:
            s["spread"][...] += part
    for t in range(NWIN):
        for pair in range(PAIRS):
            first = (WW - 1 - 2 * pair) * ZR
            rows = s["spread"][t * HEADS * STRIP : (t + 1) * HEADS * STRIP, first : first + WIN]
            s["bias"][t * HEADS : (t + 1) * HEADS, pair * STRIP : (pair + 1) * STRIP, :] = rows.reshape(
                HEADS, STRIP, WIN
            )
    s["wqkvt"][...] = w_qkv[...].T
    ccol = ccol_ref[...]
    ii = lax.broadcasted_iota(jnp.int32, (WIN, WIN), 0)
    jj = lax.broadcasted_iota(jnp.int32, (WIN, WIN), 1)
    low_i, low_j = (lax.rem(ii, WH) >= RH).astype(jnp.int32), (lax.rem(jj, WH) >= RH).astype(jnp.int32)
    open_rows = jnp.where(lax.axis_index("lat") == plan.lat - 1, 0, 1)
    top_i, top_j = lax.rem(ii // WH, WZ), lax.rem(jj // WH, WZ)
    s["bars"][0] = jnp.where((low_i == low_j) | (open_rows == 1), 0.0, MASKED)
    s["bars"][1] = jnp.where(top_i == top_j, 0.0, MASKED)
    for copy in enter:
        copy.wait_recv()

    cells = dot(order_ref[...], frame[:, :QUARTER, :].reshape(CELLS, PACK))
    s["xs"][...] = cells[:, :C]
    s["gm"][...] = cells[:, C:].astype(BF16)

    marks = jnp.concatenate(
        [
            frame[0, QUARTER : QUARTER + EXTRA, :WIN][:CH].astype(F32),
            frame[1, QUARTER : QUARTER + EXTRA, :WIN][:CH].astype(F32),
            jnp.zeros((EXTRA - WW, WIN), F32),
        ],
        axis=0,
    ).astype(BF16)
    same = dot(ccol, marks) == lax.dot_general(
        marks, ccol, (((0,), (1,)), ((), ())), preferred_element_type=F32
    )
    barred = jnp.where(same, s["bars"][0], MASKED)
    s["bars"][0] = barred
    s["bars"][1] = jnp.minimum(barred, s["bars"][1])

    normed, inv = normed_of(s["xs"][...])
    a = normed.astype(BF16)
    s["act"][...] = a
    s["q"][...] = dot(a, w_qkv[:, :C]).astype(BF16)
    s["k"][...] = dot(a, w_qkv[:, C : 2 * C]).astype(BF16)
    s["v"][...] = dot(a, w_qkv[:, 2 * C :]).astype(BF16)

    def forward(w, carry):
        at = pl.ds(pl.multiple_of(w * WIN, WIN), WIN)
        q, k = s["q"][at, :], s["k"][at, :]
        bar = s["bars"][(w == NWIN - 1).astype(jnp.int32)]
        qkvt = dot_nt(s["wqkvt"][...], s["act"][at, :]).astype(BF16)
        s["qkvt"][w] = qkvt
        for h in range(HEADS):
            score = dot_nt(q * hm[h], k) * scale + s["bias"][w * HEADS + h] + bar
            e = jnp.exp(score - jnp.max(score, axis=-1, keepdims=True))
            p = e * (1.0 / jnp.sum(e, axis=-1, keepdims=True))
            s["prob"][w * HEADS + h] = p
            head = 2 * C + h * HEAD_DIM
            s["ot"][w, h * HEAD_DIM : (h + 1) * HEAD_DIM, :] = dot_nt(
                qkvt[head : head + HEAD_DIM, :], p.astype(BF16)
            ).astype(BF16)
        return carry

    lax.fori_loop(0, NWIN, forward, 0)

    def middle(w, carry):
        at = pl.ds(pl.multiple_of(w * WIN, WIN), WIN)
        mid = (s["xs"][at, :] + dot_tn(s["ot"][w], w_proj[...])).astype(BF16).astype(F32)
        n2, inv2 = normed_of(mid)
        b = n2.astype(BF16)
        s["b"][at, :] = b
        u = dot(b, w_up[...])
        cdf = 0.5 * (1.0 + lax.erf(u * 0.7071067811865476))
        s["m"][at, :] = (u * cdf).astype(BF16)
        slope = cdf + u * jnp.exp(-0.5 * u * u) * 0.3989422804014327
        g = s["gm"][at, :]
        du = (dot(g, w_downt[...]) * slope).astype(BF16)
        s["du"][at, :] = du
        dh = (g.astype(F32) + norm_back(dot_nt(du, w_up[...]), n2, inv2)).astype(BF16)
        s["dh"][at, :] = dh
        s["dout"][at, :] = dot_nt(dh, w_proj[...]).astype(BF16)
        s["dot"][w] = dot_nt(w_proj[...], dh).astype(BF16)
        return carry

    lax.fori_loop(0, NWIN, middle, 0)
    s["early"][:, :MLP] = dot_tn(s["b"][...], s["du"][...])
    s["early"][:, MLP : 2 * MLP] = dot_tn(s["gm"][...], s["m"][...])
    proj = jnp.zeros((C, C), F32)
    for w in range(NWIN):
        proj += dot(s["ot"][w], s["dh"][w * WIN : (w + 1) * WIN, :])
    s["early"][:, 2 * MLP : 2 * MLP + C] = proj
    s["early"][:, 2 * MLP + C :] = jnp.zeros((C, ECOLS - 2 * MLP - C), F32)
    early.fill(s["early"])
    early.core_start()

    for w in range(NWIN):
        at = pl.ds(w * WIN, WIN)
        k, v, do = s["k"][at, :], s["v"][at, :], s["dout"][at, :]
        for h in range(HEADS):
            p = s["prob"][w * HEADS + h]
            dp = dot_nt(do * hm[h], v)
            ds = p * (dp - jnp.sum(p * dp, axis=-1, keepdims=True))
            dsb = ds.astype(BF16)
            first = (w * HEADS + h) * STRIP
            for pair in range(PAIRS):
                s["dcol"][pair, first : first + STRIP, :] = dsb[pair * STRIP : (pair + 1) * STRIP, :]
            low, high = h * HEAD_DIM, (h + 1) * HEAD_DIM
            kt, qt = s["qkvt"][w, C + low : C + high, :], s["qkvt"][w, low:high, :]
            s["dqkvt"][low:high, :] = (dot_nt(kt, dsb) * scale).astype(BF16)
            s["dqkvt"][C + low : C + high, :] = (dot(qt, dsb) * scale).astype(BF16)
            s["dqkvt"][2 * C + low : 2 * C + high, :] = dot(s["dot"][w, low:high, :], p.astype(BF16)).astype(BF16)
        dqkvt = s["dqkvt"][...]
        s["back"][at, :] = dot(w_qkv[...], dqkvt).T
        term = dot(dqkvt, s["act"][at, :])
        if w == 0:
            s["lsum"][...] = term
        else:
            s["lsum"][...] += term
        if w == 0:
            early.plane_start()

    grad = jnp.zeros((2 * TROWS, KCOLS), F32)
    for pair in range(PAIRS):
        grad += dot(s["dcol"][pair], tsum_ref[pair])
    grad = grad.astype(BF16)
    s["tgrad"][...] = jnp.zeros_like(s["tgrad"])
    s["tgrad"][:, :TCOLS] = dot_nt(dot(near["even_row"][...], grad).astype(BF16), near["even_lane"][...]) + dot_nt(
        dot(near["odd_row"][...], grad).astype(BF16), near["odd_lane"][...]
    )
    s["late"][:, : 3 * C] = s["lsum"][...].T
    s["late"][:, 3 * C :] = jnp.zeros((C, LCOLS - 3 * C), F32)
    late.fill(s["late"], s["tgrad"])
    late.core_start()

    normed, inv = normed_of(s["xs"][...])
    dxs = (s["dh"][...].astype(F32) + norm_back(s["back"][...], normed, inv)).astype(BF16)
    s["send"][...] = dot(back_ref[...], dxs).astype(BF16).reshape(4, QUARTER, C)
    home = [
        remote(s["send"].at[1], s["hrecv"].at[2], hs.at[0], hr.at[0], after[0]),
        remote(s["send"].at[2], s["hrecv"].at[1], hs.at[1], hr.at[1], after[1]),
        remote(s["send"].at[3], s["hrecv"].at[0], hs.at[2], hr.at[2], after[2]),
    ]
    late.plane_start()
    for copy in home:
        copy.start()
    home_ref[3] = s["send"][0]

    early.z_start()
    late.z_start()
    early.z_back()
    late.z_back()
    early.plane_back()
    late.plane_back()
    early.hand_over()
    for copy in home:
        copy.wait_recv()
    for q in range(3):
        home_ref[q] = s["hrecv"][q]
    late.hand_over()
    early.finish()
    write_out = [pltpu.make_async_copy(early.wall, early_ref, outs.at[0])]
    write_out[0].start()
    late.finish()
    write_out.append(pltpu.make_async_copy(late.wall, late_ref, outs.at[1]))
    write_out.append(pltpu.make_async_copy(late.tall, tall_ref, outs.at[2]))
    write_out[1].start()
    write_out[2].start()
    for copy in enter + home:
        copy.wait_send()
    early.drain()
    late.drain()
    for copy in write_out:
        copy.wait()


def block(plan, state, cotangent, valid, table, w_qkv, w_proj, w_up, w_down):
    vmem = pl.BlockSpec(memory_space=pltpu.VMEM)
    hbm = pl.BlockSpec(memory_space=pl.ANY)
    order = cell_order()
    sums = (Sum(plan, ECOLS, False), Sum(plan, LCOLS, True))
    consts = (
        order, order.T, table_rows(0).T, table_rows(1).T, table_lanes(0), table_lanes(1),
        table_sums(), column_of_cell(),
    )
    far = [w_qkv, w_proj, w_up, w_down.T] + [jnp.asarray(m, BF16) for m in consts]
    scratch = [pltpu.VMEM(v.shape, v.dtype) for v in far]
    scratch += [pltpu.VMEM(shape, dtype) for shape, dtype in SCRATCH.values()]
    sem = pltpu.SemaphoreType.DMA
    scratch += [sem((len(FAR),)), sem((3,)), sem((3,)), sem((3,)), sem((3,)), sem((3,))]
    for one in sums:
        scratch += one.scratch()
    rows = lambda v: v.transpose(1, 0, 2).reshape(WH * LEVELS, WW * C)
    return pl.pallas_call(
        functools.partial(block_kernel, plan, sums),
        out_shape=[jax.ShapeDtypeStruct((4, QUARTER, C), BF16)] + sums[0].out_shapes() + sums[1].out_shapes(),
        in_specs=[vmem, vmem, pl.BlockSpec(memory_space=pltpu.SMEM), vmem, vmem] + [hbm] * len(far),
        out_specs=[vmem, hbm, hbm, hbm],
        scratch_shapes=scratch,
        compiler_params=pltpu.CompilerParams(
            collective_id=0, has_side_effects=True, vmem_limit_bytes=VMEM_LIMIT
        ),
        name="block",
    )(
        rows(state), rows(cotangent), valid.reshape(1, WW), jnp.asarray(slab_order(), BF16), table, *far
    )


def write_kernel(
    plan, factor, home_ref, early_ref, late_ref, tall_ref, slab_ref,
    dx_ref, qkv_ref, proj_ref, up_ref, down_ref, table_ref, band, early, late, tgrad,
):
    jobs = (
        (early_ref, early, ECOLS // 128, C // 16, plan.plane, factor),
        (late_ref, late, LCOLS // 128, C // 16, plan.plane, factor),
        (tall_ref, tgrad, TLANES, TROWS // 16, XL, 1.0),
    )
    for src, dst, lanes, rows, parts, gain in jobs:
        tiles = src.shape[2]
        for i in range(rows * lanes):
            core, rest = divmod(i, parts * tiles)
            r, l = divmod(i, lanes)
            value = src[core, rest // tiles, rest % tiles].astype(F32)
            dst[r * 16 : r * 16 + 16, l * 128 : l * 128 + 128] = value * gain if gain != 1.0 else value
    up_ref[...] = early[:, :MLP]
    down_ref[...] = early[:, MLP : 2 * MLP]
    proj_ref[...] = early[:, 2 * MLP : 2 * MLP + C]
    qkv_ref[...] = late[:, : 3 * C]
    for h in range(HEADS):
        for zi in range(WZ):
            for zj in range(WZ):
                for ri in range(WH):
                    seg = ((h * WZ + zi) * WZ + zj) * WH + ri
                    row = (h * ZR + zi * WH + ri) * NWIN
                    table_ref[:, seg * TSEG : (seg + 1) * TSEG] = tgrad[
                        row : row + NWIN, zj * TSEG : (zj + 1) * TSEG
                    ]
    for c in range(WW):
        for rs in range(2):
            band[rs * SLAB : (rs + 1) * SLAB, c * C : (c + 1) * C] = home_ref[
                rs * 2 + c // CH, (c % CH) * SLAB : (c % CH + 1) * SLAB, :
            ].astype(F32)
    dx_ref[...] = dot(slab_ref[...], band[...].astype(BF16)).astype(BF16)


def write(plan, home, early, late, tall):
    vmem = pl.BlockSpec(memory_space=pltpu.VMEM)
    factor = float(CELLS * plan.lon * plan.lat) ** (-0.5)
    dx, qkv, proj, up, down, table = pl.pallas_call(
        functools.partial(write_kernel, plan, factor),
        out_shape=(
            jax.ShapeDtypeStruct((WH * LEVELS, WW * C), BF16),
            jax.ShapeDtypeStruct((C, 3 * C), F32),
            jax.ShapeDtypeStruct((C, C), F32),
            jax.ShapeDtypeStruct((C, MLP), F32),
            jax.ShapeDtypeStruct((C, MLP), F32),
            jax.ShapeDtypeStruct((NWIN, HEADS * ZR * ZR * SPAN), F32),
        ),
        in_specs=[vmem] * 5,
        out_specs=(vmem,) * 6,
        scratch_shapes=[
            pltpu.VMEM((2 * SLAB, WW * C), F32),
            pltpu.VMEM((C, ECOLS), F32),
            pltpu.VMEM((C, LCOLS), F32),
            pltpu.VMEM((TROWS, TLANES * 128), F32),
        ],
        compiler_params=pltpu.CompilerParams(vmem_limit_bytes=VMEM_LIMIT),
        name="write",
    )(home, early, late, tall, jnp.asarray(slab_order().T, BF16))
    dx = dx.reshape(WH, LEVELS, WW * C).transpose(1, 0, 2)
    return dx, qkv, proj, up, down.T, table


def per_device(plan, state_in, cotangent, w_qkv, w_proj, w_up, w_down, bias_table, pad_valid):
    return write(plan, *block(plan, state_in, cotangent, pad_valid, bias_table, w_qkv, w_proj, w_up, w_down))


def solution(mesh):
    plan = Plan(mesh.shape["lon"], mesh.shape["lat"])
    return jax.shard_map(
        functools.partial(per_device, plan),
        mesh=mesh,
        in_specs=(
            P(None, "lat", "lon"),
            P(None, "lat", "lon"),
            P(),
            P(),
            P(),
            P(),
            P("lat", None),
            P("lon"),
        ),
        out_specs=(P(None, "lat", "lon"), P(), P(), P(), P(), P("lat", None)),
        check_vma=False,
    )
```

```python
import functools

import jax
import jax.numpy as jnp
import numpy as np
from jax import lax
from jax.experimental import pallas as pl
from jax.experimental.pallas import tpu as pltpu
from jax.sharding import PartitionSpec as P

F32 = jnp.float32
BF16 = jnp.bfloat16
MESH = pl.DeviceIdType.MESH

C = 192
HEADS = 6
HEAD_DIM = 32
MLP = 768
WZ = 2
WH = 6
WW = 12
LEVELS = 8
WIN = WZ * WH * WW
NWIN = LEVELS // WZ
CELLS = WIN * NWIN
CH = WW // 2
RH = WH // 2
SLAB = LEVELS * RH
QUARTER = CH * SLAB
PACK = 2 * C
EXTRA = 16
SPAN = 2 * WW - 1
ZR = WZ * WH
PAIRS = WW // 2
STRIP = 2 * ZR
TROWS = NWIN * HEADS * ZR
TCOLS = ZR * SPAN
TSEG = WH * SPAN
DOWN = 512
ECOLS = MLP + DOWN
LCOLS = 4 * C + MLP - DOWN
KCOLS = (SPAN + 1) * ZR
TLANES = -(-TCOLS // 128)
TTILES = (TROWS // 16) * TLANES
XL = 2
NORM_EPS = 1e-5
MASKED = -1e30
VMEM_LIMIT = 56 * 1024 * 1024


def up_to(value, unit):
    return -(-value // unit) * unit


class Plan:
    def __init__(self, lon, lat):
        self.lon, self.lat = lon, lat
        self.nz = lon // (2 * XL)
        self.plane = XL * lat
        self.tt = -(-TTILES // (2 * XL))
        self.trows = self.tt * 16 // self.nz
        assert self.trows * self.nz == self.tt * 16

    def weight_tiles(self, columns):
        tiles = -(-(C // 16) * (columns // 128) // (2 * self.plane))
        while tiles * 16 % self.nz:
            tiles += 1
        return tiles


def cell_order():
    perm = np.zeros((CELLS, CELLS), np.float32)
    for w in range(NWIN):
        for c in range(WW):
            for z in range(WZ):
                for r in range(WH):
                    row = w * WIN + c * ZR + z * WH + r
                    quarter = (r // RH) * 2 + c // CH
                    col = quarter * QUARTER + (c % CH) * SLAB + w * WZ * RH + z * RH + r % RH
                    perm[row, col] = 1
    return perm


def slab_order():
    perm = np.zeros((2 * SLAB, LEVELS * WH), np.float32)
    for rs in range(2):
        for w in range(NWIN):
            for z in range(WZ):
                for r in range(RH):
                    row = rs * SLAB + w * WZ * RH + z * RH + r
                    perm[row, (rs * RH + r) * LEVELS + (2 * w + z + WZ // 2) % LEVELS] = 1
    return perm


def table_lanes(odd):
    perm = np.zeros((TCOLS, KCOLS), np.float32)
    for b in range(ZR):
        for d in range(SPAN):
            perm[b * SPAN + d, (SPAN - 1 - d + odd) * ZR + b] = 1
    return perm


def table_sums():
    hit = np.zeros((PAIRS, WIN, KCOLS), np.float32)
    for pair in range(PAIRS):
        for cj in range(WW):
            for b in range(ZR):
                hit[pair, cj * ZR + b, (cj - 2 * pair + WW - 1) * ZR + b] = 1
    return hit


def column_of_cell():
    hit = np.zeros((WIN, EXTRA), np.float32)
    for c in range(WW):
        hit[c * ZR : (c + 1) * ZR, c] = 1
    return hit


def segments(h, zi, ri):
    return [(((h * WZ + zi) * WZ + zj) * WH + ri) * TSEG for zj in range(WZ)]


def dot(a, b):
    return lax.dot_general(a, b, (((1,), (0,)), ((), ())), preferred_element_type=F32)


def dot_nt(a, b):
    return lax.dot_general(a, b, (((1,), (1,)), ((), ())), preferred_element_type=F32)


def dot_tn(a, b):
    return lax.dot_general(a, b, (((0,), (0,)), ((), ())), preferred_element_type=F32)


def neighbours(plan):
    lon, lat = lax.axis_index("lon"), lax.axis_index("lat")
    lon_b, lon_a = lax.rem(lon + plan.lon - 1, plan.lon), lax.rem(lon + 1, plan.lon)
    lat_b, lat_a = lax.rem(lat + plan.lat - 1, plan.lat), lax.rem(lat + 1, plan.lat)
    before = [(lon_b, lat), (lon, lat_b), (lon_b, lat_b)]
    after = [(lon_a, lat), (lon, lat_a), (lon_a, lat_a)]
    return before, after


def remote(src, dst, send, recv, place):
    return pltpu.make_async_remote_copy(
        src_ref=src, dst_ref=dst, send_sem=send, recv_sem=recv,
        device_id={"lon": place[0], "lat": place[1]}, device_id_type=MESH,
    )


def greet(place):
    pl.semaphore_signal(
        pltpu.get_barrier_semaphore(), inc=1,
        device_id={"lon": place[0], "lat": place[1]}, device_id_type=MESH,
    )


def each(first, last, act):
    def step(i, carry):
        act(i)
        return carry

    lax.fori_loop(first, last, step, 0)


class Spot:
    def __init__(self, plan):
        self.plan = plan
        self.lon, self.lat = lax.axis_index("lon"), lax.axis_index("lat")
        self.nz, self.plane = plan.nz, plan.plane
        self.core = lax.rem(self.lon, 2)
        self.z = lax.rem(self.lon // 2, self.nz)
        self.xl = self.lon // (2 * self.nz)
        self.me = self.xl * plan.lat + self.lat
        self.other = self.at(self.me, self.z, 1 - self.core)
        self.across = self.at((1 - self.xl) * plan.lat + self.lat, self.z, self.core)

    def at(self, p, z, core):
        return (p // self.plan.lat) * (2 * self.nz) + z * 2 + core, lax.rem(p, self.plan.lat)

    def at_plane(self, p):
        return self.at(p, self.z, self.core)

    def at_z(self, z):
        return self.at(self.me, z, self.core)

    def plane_peer(self, d):
        return lax.rem(self.me + d, self.plane)

    def z_peer(self, d):
        return lax.rem(self.z + d, self.nz)

    def greet_all(self):
        greet(self.other)
        each(1, self.plane, lambda d: greet(self.at_plane(self.plane_peer(d))))
        each(1, self.nz, lambda d: greet(self.at_z(self.z_peer(d))))
        return 1 + self.plane - 1 + self.nz - 1


def cut(src, out, lanes, rows, parts, tiles):
    for i in range(2 * parts * tiles):
        core, rest = divmod(i, parts * tiles)
        place = (core, rest // tiles, rest % tiles)
        if i < rows * lanes:
            r, l = divmod(i, lanes)
            out[place] = src[r * 16 : r * 16 + 16, l * 128 : l * 128 + 128].astype(BF16)
        else:
            out[place] = jnp.zeros((16, 128), BF16)


def all_in(held, sem, place):
    remote(held, held, sem, sem, place).wait_recv()


def all_out(held, sem, place):
    remote(held, held, sem, sem, place).wait_send()


def tile_sum(a, b):
    return a.astype(F32) + b.astype(F32)


class Bound:
    def shapes(self):
        raise NotImplementedError

    def scratch(self):
        shapes = self.shapes()
        self.names = list(shapes)
        return list(shapes.values())

    def bind(self, spot, refs):
        self.spot = spot
        for name, ref in zip(self.names, refs):
            setattr(self, name, ref)


class OverZ(Bound):
    def z_shapes(self, lines, nz):
        sem = pltpu.SemaphoreType.DMA
        self.zlen = lines // nz
        self.zpad = up_to(self.zlen, 16)
        piece = (nz, self.zpad, 128)
        return dict(
            rows=pltpu.VMEM((lines, 128), F32), zrows=pltpu.VMEM(piece, F32),
            zsend=pltpu.VMEM(piece, BF16), zrecv=pltpu.VMEM(piece, BF16), zall=pltpu.VMEM(piece, BF16),
            z1s=sem((1,)), z1r=sem((1,)), z2s=sem((1,)), z2r=sem((1,)),
        )

    def z_send_rows(self):
        s, n = self.spot, self.zlen
        if n < self.zpad:
            self.zrows[...] = jnp.zeros_like(self.zrows)
        for i in range(s.nz):
            self.zrows[i, :n, :] = self.rows[i * n : (i + 1) * n, :]
        self.zsend[...] = self.zrows[...].astype(BF16)

        def send(d):
            p = s.z_peer(d)
            remote(self.zsend.at[p], self.zrecv.at[d], self.z1s.at[0], self.z1r.at[0], s.at_z(p)).start()

        each(1, s.nz, send)

    def z_back(self):
        s = self.spot
        rest = pl.ds(1, s.nz - 1)
        all_in(self.zrecv.at[rest], self.z1r.at[0], s.other)
        total = self.zsend[s.z].astype(F32)
        for d in range(1, s.nz):
            total = total + self.zrecv[d].astype(F32)
        self.zall[s.z] = total.astype(BF16)
        mine = self.zall.at[s.z]
        each(1, s.nz, lambda d: remote(mine, mine, self.z2s.at[0], self.z2r.at[0], s.at_z(s.z_peer(d))).start())

    def z_take_rows(self):
        s, n = self.spot, self.zlen
        rest = pl.ds(1, s.nz - 1)
        all_in(self.zall.at[rest], self.z2r.at[0], s.other)
        self.zrows[...] = self.zall[...].astype(F32)
        for i in range(s.nz):
            self.rows[i * n : (i + 1) * n, :] = self.zrows[i, :n, :]

    def z_drain(self):
        rest = pl.ds(1, self.spot.nz - 1)
        all_out(self.zsend.at[rest], self.z1s.at[0], self.spot.other)
        all_out(self.zall.at[rest], self.z2s.at[0], self.spot.other)


class WeightSum(OverZ):
    def __init__(self, plan, columns, whole):
        self.plan, self.columns, self.whole = plan, columns, whole
        self.wt = plan.weight_tiles(columns)

    def out_shape(self):
        return jax.ShapeDtypeStruct((2, self.plan.plane, self.wt, 16, 128), BF16)

    def shapes(self):
        plane, nz, wt = self.plan.plane, self.plan.nz, self.wt
        sem = pltpu.SemaphoreType.DMA
        full, half = (2, plane, wt, 16, 128), (plane, wt, 16, 128)
        shapes = dict(
            wsend=pltpu.VMEM(full, BF16), wr1=pltpu.VMEM(half, BF16), w1=pltpu.VMEM(half, BF16),
            wr2=pltpu.VMEM(half, BF16), wall=pltpu.VMEM(full, BF16),
            c1s=sem((1,)), c1r=sem((1,)), p2s=sem((1,)), p2r=sem((1,)),
            p3s=sem((1,)), p3r=sem((1,)), c4s=sem((1,)), c4r=sem((1,)),
        )
        if self.whole:
            shapes.update(zrecv=pltpu.VMEM((nz, wt, 16, 128), BF16), z1s=sem((1,)), z1r=sem((1,)))
        else:
            shapes.update(self.z_shapes(wt * 16, nz))
        return shapes

    def core_copy(self):
        s = self.spot
        return remote(self.wsend.at[1 - s.core], self.wr1, self.c1s.at[0], self.c1r.at[0], s.other)

    def hand(self):
        s = self.spot
        held = self.wall.at[s.core]
        return remote(held, held, self.c4s.at[0], self.c4r.at[0], s.other)

    def fill(self, total):
        cut(total, self.wsend, self.columns // 128, C // 16, self.plan.plane, self.wt)

    def core_start(self):
        self.core_copy().start()

    def plane_start(self):
        s = self.spot
        self.core_copy().wait_recv()
        self.w1[...] = tile_sum(self.wsend[s.core], self.wr1[...]).astype(BF16)

        def send(d):
            p = s.plane_peer(d)
            remote(self.w1.at[p], self.wr2.at[d], self.p2s.at[0], self.p2r.at[0], s.at_plane(p)).start()

        each(1, s.plane, send)

    def z_start(self):
        s = self.spot
        all_in(self.wr2.at[pl.ds(1, s.plane - 1)], self.p2r.at[0], s.other)
        total = tile_sum(self.wsend[s.core, s.me], self.wr1[s.me])
        for d in range(1, s.plane):
            total = total + self.wr2[d].astype(F32)
        if self.whole:
            self.zrecv[s.z] = total.astype(BF16)
            mine = self.zrecv.at[s.z]
            each(1, s.nz, lambda d: remote(mine, mine, self.z1s.at[0], self.z1r.at[0], s.at_z(s.z_peer(d))).start())
        else:
            self.rows[...] = total.reshape(self.wt * 16, 128)
            self.z_send_rows()

    def plane_back(self):
        s = self.spot
        if self.whole:
            all_in(self.zrecv.at[pl.ds(1, s.nz - 1)], self.z1r.at[0], s.other)
            total = self.zrecv[0].astype(F32)
            for i in range(1, s.nz):
                total = total + self.zrecv[i].astype(F32)
        else:
            self.z_take_rows()
            total = self.rows[...].reshape(self.wt, 16, 128)
        self.wall[s.core, s.me] = total.astype(BF16)
        mine = self.wall.at[s.core, s.me]
        each(
            1, s.plane,
            lambda d: remote(mine, mine, self.p3s.at[0], self.p3r.at[0], s.at_plane(s.plane_peer(d))).start(),
        )

    def hand_over(self):
        s = self.spot
        all_in(self.wall.at[s.core, pl.ds(1, s.plane - 1)], self.p3r.at[0], s.other)
        self.hand().start()

    def finish(self):
        self.hand().wait_recv()

    def drain(self):
        s = self.spot
        rest = pl.ds(1, s.plane - 1)
        self.core_copy().wait_send()
        all_out(self.w1.at[rest], self.p2s.at[0], s.other)
        all_out(self.wall.at[s.core, rest], self.p3s.at[0], s.other)
        if self.whole:
            all_out(self.zrecv.at[pl.ds(1, s.nz - 1)], self.z1s.at[0], s.other)
        else:
            self.z_drain()
        self.hand().wait_send()


class TableSum(OverZ):
    def __init__(self, plan):
        self.plan = plan

    def out_shape(self):
        return jax.ShapeDtypeStruct((2, XL, self.plan.tt, 16, 128), BF16)

    def shapes(self):
        tt, nz = self.plan.tt, self.plan.nz
        sem = pltpu.SemaphoreType.DMA
        full, half, part = (2, XL, tt, 16, 128), (XL, tt, 16, 128), (tt, 16, 128)
        shapes = dict(
            tsend=pltpu.VMEM(full, BF16), tr1=pltpu.VMEM(half, BF16), t1=pltpu.VMEM(part, BF16),
            tr2=pltpu.VMEM(part, BF16), wall=pltpu.VMEM(full, BF16),
            send=sem((5,)), recv=sem((5,)),
        )
        shapes.update(self.z_shapes(tt * 16, nz))
        return shapes

    def copies(self, n):
        s = self.spot
        if n == 0:
            src, dst, place = self.tsend.at[1 - s.core], self.tr1, s.other
        elif n == 1:
            src, dst, place = self.t1, self.tr2, s.across
        else:
            src = dst = self.wall.at[s.core, 1 - s.xl if n == 4 else s.xl]
            place = s.across if n == 2 else s.other
        return remote(src, dst, self.send.at[n], self.recv.at[n], place)

    def fill(self, total):
        cut(total, self.tsend, TLANES, TROWS // 16, XL, self.plan.tt)

    def core_start(self):
        self.copies(0).start()

    def pair_start(self):
        s = self.spot
        self.copies(0).wait_recv()
        far = 1 - s.xl
        self.t1[...] = tile_sum(self.tsend[s.core, far], self.tr1[far]).astype(BF16)
        self.copies(1).start()

    def z_start(self):
        s = self.spot
        near = tile_sum(self.tsend[s.core, s.xl], self.tr1[s.xl])
        self.copies(1).wait_recv()
        self.rows[...] = (near + self.tr2[...].astype(F32)).reshape(self.plan.tt * 16, 128)
        self.z_send_rows()

    def pair_back(self):
        s = self.spot
        self.z_take_rows()
        self.wall[s.core, s.xl] = self.rows[...].astype(BF16).reshape(self.plan.tt, 16, 128)
        self.copies(2).start()
        self.copies(3).start()

    def hand_over(self):
        self.copies(2).wait_recv()
        self.copies(4).start()

    def finish(self):
        self.copies(3).wait_recv()
        self.copies(4).wait_recv()

    def drain(self):
        for n in range(5):
            self.copies(n).wait_send()
        self.z_drain()


def normed_of(v):
    centred = v - jnp.mean(v, axis=-1, keepdims=True)
    inv = lax.rsqrt(jnp.mean(centred * centred, axis=-1, keepdims=True) + NORM_EPS)
    return centred * inv, inv


def norm_back(up, normed, inv):
    return inv * (
        up
        - jnp.mean(up, axis=-1, keepdims=True)
        - normed * jnp.mean(up * normed, axis=-1, keepdims=True)
    )


FAR = (
    "w_qkv", "w_proj", "w_up", "w_downt", "order", "back",
    "even_lane", "odd_lane", "tsum", "ccol",
)
LANES = ("even_lane", "odd_lane")
QUARTERS = (4, QUARTER + EXTRA, PACK)
SCRATCH = dict(
    packed=(QUARTERS, F32),
    outward=(QUARTERS, BF16),
    frame=(QUARTERS, BF16),
    tn=((TLANES, TROWS, 128), F32),
    lined=((2, TROWS, KCOLS), F32),
    spread=((2 * TROWS, KCOLS), F32),
    bars=((2, WIN, WIN), F32),
    xs=((CELLS, C), F32),
    gm=((CELLS, C), BF16),
    act=((CELLS, C), BF16),
    q=((CELLS, C), BF16),
    k=((CELLS, C), BF16),
    v=((CELLS, C), BF16),
    qkvt=((NWIN, 3 * C, WIN), BF16),
    ot=((NWIN, C, WIN), BF16),
    dot=((NWIN, C, WIN), BF16),
    dh=((CELLS, C), BF16),
    dout=((CELLS, C), BF16),
    b=((CELLS, C), BF16),
    m=((CELLS, MLP), BF16),
    du=((CELLS, MLP), BF16),
    dqkvt=((3 * C, WIN), BF16),
    back=((CELLS, C), F32),
    wqkvt=((3 * C, C), BF16),
    bias=((NWIN * HEADS, WIN, WIN), F32),
    prob=((NWIN * HEADS, WIN, WIN), F32),
    probb=((NWIN * HEADS, WIN, WIN), BF16),
    dcol=((PAIRS, 2 * TROWS, WIN), F32),
    early=((C, ECOLS), F32),
    late=((C, LCOLS), F32),
    lsum=((3 * C, C), F32),
    tgrad=((TROWS, TLANES * 128), F32),
    send=((4, QUARTER, C), BF16),
    hrecv=((4, QUARTER, C), BF16),
)


def block_kernel(plan, sums, *refs):
    x_ref, g_ref, valid_ref, slab_ref, table_ref = refs[:5]
    far = refs[5 : 5 + len(FAR)]
    refs = refs[5 + len(FAR) :]
    home_ref, early_ref, late_ref, tall_ref = refs[:4]
    near = dict(zip(FAR, refs[4 : 4 + len(FAR)]))
    refs = refs[4 + len(FAR) :]
    s = dict(zip(SCRATCH, refs))
    refs = refs[len(SCRATCH) :]
    fs, es, er, hs, hr, outs = refs[:6]
    refs = refs[6:]
    spot = Spot(plan)
    early, late, table = sums
    for one in sums:
        one.bind(spot, refs[: len(one.names)])
        refs = refs[len(one.names) :]
    before, after = neighbours(plan)
    for place in before + after:
        greet(place)
    greeted = spot.greet_all() + 6
    fetch = [pltpu.make_async_copy(src, near[name], fs.at[n]) for n, (name, src) in enumerate(zip(FAR, far))]
    for copy in fetch:
        copy.start()
    w_qkv, w_proj, w_up, w_downt, order_ref, back_ref, tsum_ref, ccol_ref = (
        near[n] for n in ("w_qkv", "w_proj", "w_up", "w_downt", "order", "back", "tsum", "ccol")
    )

    hm = []
    lane = lax.broadcasted_iota(jnp.int32, (1, C), 1)
    for h in range(HEADS):
        hm.append(jnp.where(lane // HEAD_DIM == h, 1.0, 0.0).astype(BF16))
    scale = HEAD_DIM ** (-0.5)

    slab = slab_ref[...]
    packed, outward, frame = s["packed"], s["outward"], s["frame"]
    packed[:, QUARTER:, :] = jnp.zeros((4, EXTRA, PACK), F32)
    for part, ref in enumerate((x_ref, g_ref)):
        rows = dot(slab, ref[...])
        for c in range(WW):
            for rs in range(2):
                piece = rows[rs * SLAB : (rs + 1) * SLAB, c * C : (c + 1) * C]
                if part == 1:
                    piece = piece * valid_ref[0, c].astype(F32)
                packed[
                    rs * 2 + c // CH, (c % CH) * SLAB : (c % CH + 1) * SLAB, part * C : (part + 1) * C
                ] = piece
    for c in range(WW):
        mark = jnp.full((1, PACK), valid_ref[0, c].astype(F32), F32)
        for rs in range(2):
            packed[rs * 2 + c // CH, QUARTER + c % CH : QUARTER + c % CH + 1, :] = mark
    outward[...] = packed[...].astype(BF16)
    blank = jnp.zeros((NWIN, TLANES * 128 - TCOLS), F32)
    for h in range(HEADS):
        for zi in range(WZ):
            for ri in range(WH):
                pieces = [table_ref[:, at : at + TSEG] for at in segments(h, zi, ri)]
                line = jnp.concatenate(pieces + [blank], axis=1)
                rows = pl.ds(h * ZR + zi * WH + ri, NWIN, stride=HEADS * ZR)
                for l in range(TLANES):
                    s["tn"][l, rows, :] = line[:, l * 128 : (l + 1) * 128]
    pl.semaphore_wait(pltpu.get_barrier_semaphore(), greeted)
    enter = [
        remote(outward.at[2], frame.at[1], es.at[0], er.at[0], before[0]),
        remote(outward.at[1], frame.at[2], es.at[1], er.at[1], before[1]),
        remote(outward.at[0], frame.at[3], es.at[2], er.at[2], before[2]),
    ]
    for copy in enter:
        copy.start()
    frame[0] = outward[3]

    for copy in fetch:
        copy.wait()
    left = jnp.concatenate([s["tn"][l] for l in range(TLANES)], axis=1)[:, :TCOLS]
    for n in range(3):
        term = left.astype(BF16)
        left = left - term.astype(F32)
        for odd in range(2):
            part = dot(term, near[LANES[odd]][...])
            if n == 0:
                s["lined"][odd] = part
            else:
                s["lined"][odd] += part
    for i in range(NWIN * HEADS):
        for odd in range(2):
            s["spread"][i * STRIP + odd * ZR : i * STRIP + (odd + 1) * ZR, :] = s["lined"][
                odd, i * ZR : (i + 1) * ZR, :
            ]
    for t in range(NWIN):
        for pair in range(PAIRS):
            first = (WW - 1 - 2 * pair) * ZR
            rows = s["spread"][t * HEADS * STRIP : (t + 1) * HEADS * STRIP, first : first + WIN]
            s["bias"][t * HEADS : (t + 1) * HEADS, pair * STRIP : (pair + 1) * STRIP, :] = rows.reshape(
                HEADS, STRIP, WIN
            )
    s["wqkvt"][...] = w_qkv[...].T
    ccol = ccol_ref[...]
    ii = lax.broadcasted_iota(jnp.int32, (WIN, WIN), 0)
    jj = lax.broadcasted_iota(jnp.int32, (WIN, WIN), 1)
    low_i, low_j = (lax.rem(ii, WH) >= RH).astype(jnp.int32), (lax.rem(jj, WH) >= RH).astype(jnp.int32)
    open_rows = jnp.where(lax.axis_index("lat") == plan.lat - 1, 0, 1)
    top_i, top_j = lax.rem(ii // WH, WZ), lax.rem(jj // WH, WZ)
    s["bars"][0] = jnp.where((low_i == low_j) | (open_rows == 1), 0.0, MASKED)
    s["bars"][1] = jnp.where(top_i == top_j, 0.0, MASKED)
    for copy in enter:
        copy.wait_recv()

    cells = dot(order_ref[...], frame[:, :QUARTER, :].reshape(CELLS, PACK))
    s["xs"][...] = cells[:, :C]
    s["gm"][...] = cells[:, C:].astype(BF16)

    marks = jnp.concatenate(
        [
            frame[0, QUARTER : QUARTER + EXTRA, :WIN][:CH].astype(F32),
            frame[1, QUARTER : QUARTER + EXTRA, :WIN][:CH].astype(F32),
            jnp.zeros((EXTRA - WW, WIN), F32),
        ],
        axis=0,
    ).astype(BF16)
    same = dot(ccol, marks) == lax.dot_general(
        marks, ccol, (((0,), (1,)), ((), ())), preferred_element_type=F32
    )
    barred = jnp.where(same, s["bars"][0], MASKED)
    s["bars"][0] = barred
    s["bars"][1] = jnp.minimum(barred, s["bars"][1])

    normed, inv = normed_of(s["xs"][...])
    a = normed.astype(BF16)
    s["act"][...] = a
    s["q"][...] = dot(a, w_qkv[:, :C]).astype(BF16)
    s["k"][...] = dot(a, w_qkv[:, C : 2 * C]).astype(BF16)
    s["v"][...] = dot(a, w_qkv[:, 2 * C :]).astype(BF16)

    def forward(w, carry):
        at = pl.ds(pl.multiple_of(w * WIN, WIN), WIN)
        q, k = s["q"][at, :], s["k"][at, :]
        bar = s["bars"][(w == NWIN - 1).astype(jnp.int32)]
        qkvt = dot_nt(s["wqkvt"][...], s["act"][at, :]).astype(BF16)
        s["qkvt"][w] = qkvt
        heads = pl.ds(w * HEADS, HEADS)
        split = jnp.concatenate([q * hm[h] for h in range(HEADS)], axis=0)
        score = dot_nt(split, k).reshape(HEADS, WIN, WIN) * scale + s["bias"][heads] + bar
        e = jnp.exp(score - jnp.max(score, axis=-1, keepdims=True))
        p = e * (1.0 / jnp.sum(e, axis=-1, keepdims=True))
        s["prob"][heads] = p
        pb = p.astype(BF16)
        s["probb"][heads] = pb
        for h in range(HEADS):
            head = 2 * C + h * HEAD_DIM
            s["ot"][w, h * HEAD_DIM : (h + 1) * HEAD_DIM, :] = dot_nt(
                qkvt[head : head + HEAD_DIM, :], pb[h]
            ).astype(BF16)
        return carry

    lax.fori_loop(0, NWIN, forward, 0)

    mixed = jnp.concatenate([dot_tn(s["ot"][w], w_proj[...]) for w in range(NWIN)], axis=0)
    mid = (s["xs"][...] + mixed).astype(BF16).astype(F32)
    n2, inv2 = normed_of(mid)
    b = n2.astype(BF16)
    s["b"][...] = b
    u = dot(b, w_up[...])
    cdf = 0.5 * (1.0 + lax.erf(u * 0.7071067811865476))
    s["m"][...] = (u * cdf).astype(BF16)
    slope = cdf + u * jnp.exp(-0.5 * u * u) * 0.3989422804014327
    g = s["gm"][...]
    du = (dot(g, w_downt[...]) * slope).astype(BF16)
    s["du"][...] = du
    dh = (g.astype(F32) + norm_back(dot_nt(du, w_up[...]), n2, inv2)).astype(BF16)
    s["dh"][...] = dh
    s["dout"][...] = dot_nt(dh, w_proj[...]).astype(BF16)
    for w in range(NWIN):
        s["dot"][w] = dot_nt(w_proj[...], dh[w * WIN : (w + 1) * WIN, :]).astype(BF16)
    s["early"][:, :MLP] = dot_tn(s["b"][...], s["du"][...])
    s["early"][:, MLP:] = dot_tn(s["gm"][...], s["m"][:, :DOWN])
    early.fill(s["early"])
    early.core_start()

    for w in range(NWIN):
        at = pl.ds(w * WIN, WIN)
        k, v, do = s["k"][at, :], s["v"][at, :], s["dout"][at, :]
        split = jnp.concatenate([do * hm[h] for h in range(HEADS)], axis=0)
        dp = dot_nt(split, v).reshape(HEADS, WIN, WIN)
        p = s["prob"][w * HEADS : (w + 1) * HEADS]
        ds = p * (dp - jnp.sum(p * dp, axis=-1, keepdims=True))
        dsb = ds.astype(BF16)
        for h in range(HEADS):
            first = (w * HEADS + h) * STRIP
            for pair in range(PAIRS):
                s["dcol"][pair, first : first + STRIP, :] = ds[h, pair * STRIP : (pair + 1) * STRIP, :]
            low, high = h * HEAD_DIM, (h + 1) * HEAD_DIM
            kt, qt = s["qkvt"][w, C + low : C + high, :], s["qkvt"][w, low:high, :]
            s["dqkvt"][low:high, :] = (dot_nt(kt, dsb[h]) * scale).astype(BF16)
            s["dqkvt"][C + low : C + high, :] = (dot(qt, dsb[h]) * scale).astype(BF16)
            s["dqkvt"][2 * C + low : 2 * C + high, :] = dot(
                s["dot"][w, low:high, :], s["probb"][w * HEADS + h]
            ).astype(BF16)
        dqkvt = s["dqkvt"][...]
        s["back"][at, :] = dot(w_qkv[...], dqkvt).T
        term = dot(dqkvt, s["act"][at, :])
        if w == 0:
            s["lsum"][...] = term
        else:
            s["lsum"][...] += term
        if w == NWIN - 2:
            early.plane_start()

    grad = jnp.zeros((2 * TROWS, KCOLS), F32)
    for pair in range(PAIRS):
        grad += dot(s["dcol"][pair].astype(BF16), tsum_ref[pair])
    s["spread"][...] = grad
    for i in range(NWIN * HEADS):
        for odd in range(2):
            s["lined"][odd, i * ZR : (i + 1) * ZR, :] = s["spread"][
                i * STRIP + odd * ZR : i * STRIP + (odd + 1) * ZR, :
            ]
    s["tgrad"][:, TCOLS:] = jnp.zeros((TROWS, TLANES * 128 - TCOLS), F32)
    s["tgrad"][:, :TCOLS] = dot_nt(s["lined"][0].astype(BF16), near["even_lane"][...]) + dot_nt(
        s["lined"][1].astype(BF16), near["odd_lane"][...]
    )
    table.fill(s["tgrad"])
    table.core_start()
    s["late"][:, : 3 * C] = s["lsum"][...].T
    proj = jnp.zeros((C, C), F32)
    for w in range(NWIN):
        proj += dot(s["ot"][w], s["dh"][w * WIN : (w + 1) * WIN, :])
    s["late"][:, 3 * C : 4 * C] = proj
    s["late"][:, 4 * C :] = dot_tn(s["gm"][...], s["m"][:, DOWN:])
    late.fill(s["late"])
    late.core_start()

    normed, inv = normed_of(s["xs"][...])
    dxs = (s["dh"][...].astype(F32) + norm_back(s["back"][...], normed, inv)).astype(BF16)
    s["send"][...] = dot(back_ref[...], dxs).astype(BF16).reshape(4, QUARTER, C)
    home = [
        remote(s["send"].at[1], s["hrecv"].at[2], hs.at[0], hr.at[0], after[0]),
        remote(s["send"].at[2], s["hrecv"].at[1], hs.at[1], hr.at[1], after[1]),
        remote(s["send"].at[3], s["hrecv"].at[0], hs.at[2], hr.at[2], after[2]),
    ]
    table.pair_start()
    late.plane_start()
    for copy in home:
        copy.start()
    home_ref[3] = s["send"][0]

    early.z_start()
    table.z_start()
    late.z_start()
    early.z_back()
    table.z_back()
    early.plane_back()
    table.pair_back()
    late.plane_back()
    table.hand_over()
    for copy in home:
        copy.wait_recv()
    for q in range(3):
        home_ref[q] = s["hrecv"][q]
    early.hand_over()
    late.hand_over()
    leave = []
    for n, (one, out) in enumerate(((table, tall_ref), (early, early_ref), (late, late_ref))):
        one.finish()
        leave.append(pltpu.make_async_copy(one.wall, out, outs.at[n]))
        leave[-1].start()
    for copy in enter + home:
        copy.wait_send()
    for one in sums:
        one.drain()
    for copy in leave:
        copy.wait()


def block(plan, state, cotangent, valid, table, w_qkv, w_proj, w_up, w_down):
    vmem = pl.BlockSpec(memory_space=pltpu.VMEM)
    hbm = pl.BlockSpec(memory_space=pl.ANY)
    order = cell_order()
    sums = (WeightSum(plan, ECOLS, False), WeightSum(plan, LCOLS, True), TableSum(plan))
    consts = (
        order, order.T, table_lanes(0), table_lanes(1), table_sums(), column_of_cell(),
    )
    far = [w_qkv, w_proj, w_up, w_down.T] + [jnp.asarray(m, BF16) for m in consts]
    scratch = [pltpu.VMEM(v.shape, v.dtype) for v in far]
    scratch += [pltpu.VMEM(shape, dtype) for shape, dtype in SCRATCH.values()]
    sem = pltpu.SemaphoreType.DMA
    scratch += [sem((len(FAR),)), sem((3,)), sem((3,)), sem((3,)), sem((3,)), sem((3,))]
    for one in sums:
        scratch += one.scratch()
    rows = lambda v: v.transpose(1, 0, 2).reshape(WH * LEVELS, WW * C)
    return pl.pallas_call(
        functools.partial(block_kernel, plan, sums),
        out_shape=[jax.ShapeDtypeStruct((4, QUARTER, C), BF16)] + [one.out_shape() for one in sums],
        in_specs=[vmem, vmem, pl.BlockSpec(memory_space=pltpu.SMEM), vmem, vmem] + [hbm] * len(far),
        out_specs=[vmem, hbm, hbm, hbm],
        scratch_shapes=scratch,
        compiler_params=pltpu.CompilerParams(
            collective_id=0, has_side_effects=True, vmem_limit_bytes=VMEM_LIMIT
        ),
        name="block",
    )(
        rows(state), rows(cotangent), valid.reshape(1, WW), jnp.asarray(slab_order(), BF16), table, *far
    )


def write_kernel(
    plan, factor, home_ref, early_ref, late_ref, tall_ref, slab_ref,
    dx_ref, qkv_ref, proj_ref, up_ref, down_ref, table_ref, band, early, late, tgrad,
):
    jobs = (
        (early_ref, early, ECOLS // 128, C // 16, plan.plane, factor),
        (late_ref, late, LCOLS // 128, C // 16, plan.plane, factor),
        (tall_ref, tgrad, TLANES, TROWS // 16, XL, 1.0),
    )
    for src, dst, lanes, rows, parts, gain in jobs:
        tiles = src.shape[2]
        for i in range(rows * lanes):
            core, rest = divmod(i, parts * tiles)
            r, l = divmod(i, lanes)
            value = src[core, rest // tiles, rest % tiles].astype(F32)
            if dst is tgrad:
                dst[l, r * 16 : r * 16 + 16, :] = value
            else:
                dst[r * 16 : r * 16 + 16, l * 128 : l * 128 + 128] = value * gain
    up_ref[...] = early[:, :MLP]
    down_ref[:, :DOWN] = early[:, MLP:]
    down_ref[:, DOWN:] = late[:, 4 * C :]
    proj_ref[...] = late[:, 3 * C : 4 * C]
    qkv_ref[...] = late[:, : 3 * C]
    for h in range(HEADS):
        for zi in range(WZ):
            for ri in range(WH):
                rows = pl.ds(h * ZR + zi * WH + ri, NWIN, stride=HEADS * ZR)
                line = jnp.concatenate(
                    [tgrad[l, rows, :] for l in range(TLANES)], axis=1
                )
                for zj, at in enumerate(segments(h, zi, ri)):
                    table_ref[:, at : at + TSEG] = line[:, zj * TSEG : (zj + 1) * TSEG]
    for c in range(WW):
        for rs in range(2):
            band[rs * SLAB : (rs + 1) * SLAB, c * C : (c + 1) * C] = home_ref[
                rs * 2 + c // CH, (c % CH) * SLAB : (c % CH + 1) * SLAB, :
            ].astype(F32)
    dx_ref[...] = dot(slab_ref[...], band[...].astype(BF16)).astype(BF16)


def write(plan, home, early, late, tall):
    vmem = pl.BlockSpec(memory_space=pltpu.VMEM)
    factor = float(CELLS * plan.lon * plan.lat) ** (-0.5)
    dx, qkv, proj, up, down, table = pl.pallas_call(
        functools.partial(write_kernel, plan, factor),
        out_shape=(
            jax.ShapeDtypeStruct((WH * LEVELS, WW * C), BF16),
            jax.ShapeDtypeStruct((C, 3 * C), F32),
            jax.ShapeDtypeStruct((C, C), F32),
            jax.ShapeDtypeStruct((C, MLP), F32),
            jax.ShapeDtypeStruct((C, MLP), F32),
            jax.ShapeDtypeStruct((NWIN, HEADS * ZR * ZR * SPAN), F32),
        ),
        in_specs=[vmem] * 5,
        out_specs=(vmem,) * 6,
        scratch_shapes=[
            pltpu.VMEM((2 * SLAB, WW * C), F32),
            pltpu.VMEM((C, ECOLS), F32),
            pltpu.VMEM((C, LCOLS), F32),
            pltpu.VMEM((TLANES, TROWS, 128), F32),
        ],
        compiler_params=pltpu.CompilerParams(vmem_limit_bytes=VMEM_LIMIT),
        name="write",
    )(home, early, late, tall, jnp.asarray(slab_order().T, BF16))
    dx = dx.reshape(WH, LEVELS, WW * C).transpose(1, 0, 2)
    return dx, qkv, proj, up, down.T, table


def per_device(plan, state_in, cotangent, w_qkv, w_proj, w_up, w_down, bias_table, pad_valid):
    return write(plan, *block(plan, state_in, cotangent, pad_valid, bias_table, w_qkv, w_proj, w_up, w_down))


def solution(mesh):
    plan = Plan(mesh.shape["lon"], mesh.shape["lat"])
    return jax.shard_map(
        functools.partial(per_device, plan),
        mesh=mesh,
        in_specs=(
            P(None, "lat", "lon"),
            P(None, "lat", "lon"),
            P(),
            P(),
            P(),
            P(),
            P("lat", None),
            P("lon"),
        ),
        out_specs=(P(None, "lat", "lon"), P(), P(), P(), P(), P("lat", None)),
        check_vma=False,
    )
```

```python
import functools

import jax
import jax.numpy as jnp
import numpy as np
from jax import lax
from jax.experimental import pallas as pl
from jax.experimental.pallas import tpu as pltpu
from jax.sharding import PartitionSpec as P

F32 = jnp.float32
BF16 = jnp.bfloat16
MESH = pl.DeviceIdType.MESH

C = 192
HEADS = 6
HEAD_DIM = 32
MLP = 768
WZ = 2
WH = 6
WW = 12
LEVELS = 8
WIN = WZ * WH * WW
NWIN = LEVELS // WZ
CELLS = WIN * NWIN
CH = WW // 2
RH = WH // 2
SLAB = LEVELS * RH
QUARTER = CH * SLAB
PACK = 2 * C
EXTRA = 16
SPAN = 2 * WW - 1
ZR = WZ * WH
PAIRS = WW // 2
STRIP = 2 * ZR
TROWS = NWIN * HEADS * ZR
TCOLS = ZR * SPAN
TSEG = WH * SPAN
DOWN = 512
ECOLS = MLP + DOWN
LCOLS = 4 * C + MLP - DOWN
KCOLS = (SPAN + 1) * ZR
TLANES = -(-TCOLS // 128)
TTILES = (TROWS // 16) * TLANES
XL = 2
NORM_EPS = 1e-5
MASKED = -1e30
VMEM_LIMIT = 56 * 1024 * 1024


def up_to(value, unit):
    return -(-value // unit) * unit


class Plan:
    def __init__(self, lon, lat):
        self.lon, self.lat = lon, lat
        self.nz = lon // (2 * XL)
        self.plane = XL * lat
        self.tt = -(-TTILES // (2 * XL))
        self.trows = self.tt * 16 // self.nz
        assert self.trows * self.nz == self.tt * 16

    def weight_tiles(self, columns):
        tiles = -(-(C // 16) * (columns // 128) // (2 * self.plane))
        while tiles * 16 % self.nz:
            tiles += 1
        return tiles


def cell_order():
    perm = np.zeros((CELLS, CELLS), np.float32)
    for w in range(NWIN):
        for c in range(WW):
            for z in range(WZ):
                for r in range(WH):
                    row = w * WIN + c * ZR + z * WH + r
                    quarter = (r // RH) * 2 + c // CH
                    col = quarter * QUARTER + (c % CH) * SLAB + w * WZ * RH + z * RH + r % RH
                    perm[row, col] = 1
    return perm


def slab_order():
    perm = np.zeros((2 * SLAB, LEVELS * WH), np.float32)
    for rs in range(2):
        for w in range(NWIN):
            for z in range(WZ):
                for r in range(RH):
                    row = rs * SLAB + w * WZ * RH + z * RH + r
                    perm[row, (rs * RH + r) * LEVELS + (2 * w + z + WZ // 2) % LEVELS] = 1
    return perm


def table_lanes(odd):
    perm = np.zeros((TCOLS, KCOLS), np.float32)
    for b in range(ZR):
        for d in range(SPAN):
            perm[b * SPAN + d, (SPAN - 1 - d + odd) * ZR + b] = 1
    return perm


def table_sums():
    hit = np.zeros((PAIRS, WIN, KCOLS), np.float32)
    for pair in range(PAIRS):
        for cj in range(WW):
            for b in range(ZR):
                hit[pair, cj * ZR + b, (cj - 2 * pair + WW - 1) * ZR + b] = 1
    return hit


def column_of_cell():
    hit = np.zeros((WIN, EXTRA), np.float32)
    for c in range(WW):
        hit[c * ZR : (c + 1) * ZR, c] = 1
    return hit


def segments(h, zi, ri):
    return [(((h * WZ + zi) * WZ + zj) * WH + ri) * TSEG for zj in range(WZ)]


def dot(a, b):
    return lax.dot_general(a, b, (((1,), (0,)), ((), ())), preferred_element_type=F32)


def dot_nt(a, b):
    return lax.dot_general(a, b, (((1,), (1,)), ((), ())), preferred_element_type=F32)


def dot_tn(a, b):
    return lax.dot_general(a, b, (((0,), (0,)), ((), ())), preferred_element_type=F32)


def neighbours(plan):
    lon, lat = lax.axis_index("lon"), lax.axis_index("lat")
    lon_b, lon_a = lax.rem(lon + plan.lon - 1, plan.lon), lax.rem(lon + 1, plan.lon)
    lat_b, lat_a = lax.rem(lat + plan.lat - 1, plan.lat), lax.rem(lat + 1, plan.lat)
    before = [(lon_b, lat), (lon, lat_b), (lon_b, lat_b)]
    after = [(lon_a, lat), (lon, lat_a), (lon_a, lat_a)]
    return before, after


def remote(src, dst, send, recv, place):
    return pltpu.make_async_remote_copy(
        src_ref=src, dst_ref=dst, send_sem=send, recv_sem=recv,
        device_id={"lon": place[0], "lat": place[1]}, device_id_type=MESH,
    )


def greet(place):
    pl.semaphore_signal(
        pltpu.get_barrier_semaphore(), inc=1,
        device_id={"lon": place[0], "lat": place[1]}, device_id_type=MESH,
    )


def each(first, last, act):
    def step(i, carry):
        act(i)
        return carry

    lax.fori_loop(first, last, step, 0)


class Spot:
    def __init__(self, plan):
        self.plan = plan
        self.lon, self.lat = lax.axis_index("lon"), lax.axis_index("lat")
        self.nz, self.plane = plan.nz, plan.plane
        self.core = lax.rem(self.lon, 2)
        self.z = lax.rem(self.lon // 2, self.nz)
        self.xl = self.lon // (2 * self.nz)
        self.me = self.xl * plan.lat + self.lat
        self.other = self.at(self.xl, self.lat, self.z, 1 - self.core)
        self.across = self.at(1 - self.xl, self.lat, self.z, self.core)

    def at(self, xl, lat, z, core):
        return xl * (2 * self.nz) + z * 2 + core, lat

    def at_z(self, z):
        return self.at(self.xl, self.lat, z, self.core)

    def plane_peer(self, d):
        rows = self.plan.lat
        far = (d >= rows).astype(jnp.int32)
        lat = self.lat + d - far * rows
        lat = lat - rows * (lat >= rows).astype(jnp.int32)
        xl = self.xl + far - 2 * self.xl * far
        return xl * rows + lat, self.at(xl, lat, self.z, self.core)

    def z_peer(self, d):
        z = self.z + d
        return z - self.nz * (z >= self.nz).astype(jnp.int32)

    def greet_all(self):
        greet(self.other)
        each(1, self.plane, lambda d: greet(self.plane_peer(d)[1]))
        each(1, self.nz, lambda d: greet(self.at_z(self.z_peer(d))))
        return 1 + self.plane - 1 + self.nz - 1


def cut(src, out, lanes, rows, parts, tiles):
    for i in range(2 * parts * tiles):
        core, rest = divmod(i, parts * tiles)
        place = (core, rest // tiles, rest % tiles)
        if i < rows * lanes:
            r, l = divmod(i, lanes)
            out[place] = src[r * 16 : r * 16 + 16, l * 128 : l * 128 + 128].astype(BF16)
        else:
            out[place] = jnp.zeros((16, 128), BF16)


def all_in(held, sem, place):
    remote(held, held, sem, sem, place).wait_recv()


def all_out(held, sem, place):
    remote(held, held, sem, sem, place).wait_send()


def tile_sum(a, b):
    return a.astype(F32) + b.astype(F32)


class Bound:
    def shapes(self):
        raise NotImplementedError

    def scratch(self):
        shapes = self.shapes()
        self.names = list(shapes)
        return list(shapes.values())

    def bind(self, spot, refs):
        self.spot = spot
        for name, ref in zip(self.names, refs):
            setattr(self, name, ref)


class OverZ(Bound):
    def z_shapes(self, lines, nz):
        sem = pltpu.SemaphoreType.DMA
        self.zlen = lines // nz
        self.zpad = up_to(self.zlen, 16)
        piece = (nz, self.zpad, 128)
        return dict(
            rows=pltpu.VMEM((lines, 128), F32), zrows=pltpu.VMEM(piece, F32),
            zsend=pltpu.VMEM(piece, BF16), zrecv=pltpu.VMEM(piece, BF16), zall=pltpu.VMEM(piece, BF16),
            z1s=sem((1,)), z1r=sem((1,)), z2s=sem((1,)), z2r=sem((1,)),
        )

    def z_send_rows(self):
        s, n = self.spot, self.zlen
        if n < self.zpad:
            self.zrows[...] = jnp.zeros_like(self.zrows)
        for i in range(s.nz):
            self.zrows[i, :n, :] = self.rows[i * n : (i + 1) * n, :]
        self.zsend[...] = self.zrows[...].astype(BF16)

        def send(d):
            p = s.z_peer(d)
            remote(self.zsend.at[p], self.zrecv.at[d], self.z1s.at[0], self.z1r.at[0], s.at_z(p)).start()

        each(1, s.nz, send)

    def z_back(self):
        s = self.spot
        rest = pl.ds(1, s.nz - 1)
        all_in(self.zrecv.at[rest], self.z1r.at[0], s.other)
        total = self.zsend[s.z].astype(F32)
        for d in range(1, s.nz):
            total = total + self.zrecv[d].astype(F32)
        self.zall[s.z] = total.astype(BF16)
        mine = self.zall.at[s.z]
        each(1, s.nz, lambda d: remote(mine, mine, self.z2s.at[0], self.z2r.at[0], s.at_z(s.z_peer(d))).start())

    def z_take_rows(self):
        s, n = self.spot, self.zlen
        rest = pl.ds(1, s.nz - 1)
        all_in(self.zall.at[rest], self.z2r.at[0], s.other)
        self.zrows[...] = self.zall[...].astype(F32)
        for i in range(s.nz):
            self.rows[i * n : (i + 1) * n, :] = self.zrows[i, :n, :]

    def z_drain(self):
        rest = pl.ds(1, self.spot.nz - 1)
        all_out(self.zsend.at[rest], self.z1s.at[0], self.spot.other)
        all_out(self.zall.at[rest], self.z2s.at[0], self.spot.other)


class WeightSum(OverZ):
    def __init__(self, plan, columns, whole):
        self.plan, self.columns, self.whole = plan, columns, whole
        self.wt = plan.weight_tiles(columns)

    def out_shape(self):
        return jax.ShapeDtypeStruct((2, self.plan.plane, self.wt, 16, 128), BF16)

    def shapes(self):
        plane, nz, wt = self.plan.plane, self.plan.nz, self.wt
        sem = pltpu.SemaphoreType.DMA
        full, half = (2, plane, wt, 16, 128), (plane, wt, 16, 128)
        shapes = dict(
            wsend=pltpu.VMEM(full, BF16), wr1=pltpu.VMEM(half, BF16), w1=pltpu.VMEM(half, BF16),
            wr2=pltpu.VMEM(half, BF16), wall=pltpu.VMEM(full, BF16),
            c1s=sem((1,)), c1r=sem((1,)), p2s=sem((1,)), p2r=sem((1,)),
            p3s=sem((1,)), p3r=sem((1,)), c4s=sem((1,)), c4r=sem((1,)),
        )
        if self.whole:
            shapes.update(zrecv=pltpu.VMEM((nz, wt, 16, 128), BF16), z1s=sem((1,)), z1r=sem((1,)))
        else:
            shapes.update(self.z_shapes(wt * 16, nz))
        return shapes

    def core_copy(self):
        s = self.spot
        return remote(self.wsend.at[1 - s.core], self.wr1, self.c1s.at[0], self.c1r.at[0], s.other)

    def hand(self):
        s = self.spot
        held = self.wall.at[s.core]
        return remote(held, held, self.c4s.at[0], self.c4r.at[0], s.other)

    def fill(self, total):
        cut(total, self.wsend, self.columns // 128, C // 16, self.plan.plane, self.wt)

    def core_start(self):
        self.core_copy().start()

    def plane_start(self):
        s = self.spot
        self.core_copy().wait_recv()
        self.w1[...] = tile_sum(self.wsend[s.core], self.wr1[...]).astype(BF16)

        def send(d):
            p, place = s.plane_peer(d)
            remote(self.w1.at[p], self.wr2.at[d], self.p2s.at[0], self.p2r.at[0], place).start()

        each(1, s.plane, send)

    def z_start(self):
        s = self.spot
        all_in(self.wr2.at[pl.ds(1, s.plane - 1)], self.p2r.at[0], s.other)
        total = tile_sum(self.wsend[s.core, s.me], self.wr1[s.me])
        for d in range(1, s.plane):
            total = total + self.wr2[d].astype(F32)
        if self.whole:
            self.zrecv[s.z] = total.astype(BF16)
            mine = self.zrecv.at[s.z]
            each(1, s.nz, lambda d: remote(mine, mine, self.z1s.at[0], self.z1r.at[0], s.at_z(s.z_peer(d))).start())
        else:
            self.rows[...] = total.reshape(self.wt * 16, 128)
            self.z_send_rows()

    def plane_back(self):
        s = self.spot
        if self.whole:
            all_in(self.zrecv.at[pl.ds(1, s.nz - 1)], self.z1r.at[0], s.other)
            total = self.zrecv[0].astype(F32)
            for i in range(1, s.nz):
                total = total + self.zrecv[i].astype(F32)
        else:
            self.z_take_rows()
            total = self.rows[...].reshape(self.wt, 16, 128)
        self.wall[s.core, s.me] = total.astype(BF16)
        mine = self.wall.at[s.core, s.me]
        each(
            1, s.plane,
            lambda d: remote(mine, mine, self.p3s.at[0], self.p3r.at[0], s.plane_peer(d)[1]).start(),
        )

    def hand_over(self):
        s = self.spot
        all_in(self.wall.at[s.core, pl.ds(1, s.plane - 1)], self.p3r.at[0], s.other)
        self.hand().start()

    def finish(self):
        self.hand().wait_recv()

    def drain(self):
        s = self.spot
        rest = pl.ds(1, s.plane - 1)
        self.core_copy().wait_send()
        all_out(self.w1.at[rest], self.p2s.at[0], s.other)
        all_out(self.wall.at[s.core, rest], self.p3s.at[0], s.other)
        if self.whole:
            all_out(self.zrecv.at[pl.ds(1, s.nz - 1)], self.z1s.at[0], s.other)
        else:
            self.z_drain()
        self.hand().wait_send()


class TableSum(OverZ):
    def __init__(self, plan):
        self.plan = plan

    def out_shape(self):
        return jax.ShapeDtypeStruct((2, XL, self.plan.tt, 16, 128), BF16)

    def shapes(self):
        tt, nz = self.plan.tt, self.plan.nz
        sem = pltpu.SemaphoreType.DMA
        full, half, part = (2, XL, tt, 16, 128), (XL, tt, 16, 128), (tt, 16, 128)
        shapes = dict(
            tsend=pltpu.VMEM(full, BF16), tr1=pltpu.VMEM(half, BF16), t1=pltpu.VMEM(part, BF16),
            tr2=pltpu.VMEM(part, BF16), wall=pltpu.VMEM(full, BF16),
            send=sem((5,)), recv=sem((5,)),
        )
        shapes.update(self.z_shapes(tt * 16, nz))
        return shapes

    def copies(self, n):
        s = self.spot
        if n == 0:
            src, dst, place = self.tsend.at[1 - s.core], self.tr1, s.other
        elif n == 1:
            src, dst, place = self.t1, self.tr2, s.across
        else:
            src = dst = self.wall.at[s.core, 1 - s.xl if n == 4 else s.xl]
            place = s.across if n == 2 else s.other
        return remote(src, dst, self.send.at[n], self.recv.at[n], place)

    def fill(self, total):
        cut(total, self.tsend, TLANES, TROWS // 16, XL, self.plan.tt)

    def core_start(self):
        self.copies(0).start()

    def pair_start(self):
        s = self.spot
        self.copies(0).wait_recv()
        far = 1 - s.xl
        self.t1[...] = tile_sum(self.tsend[s.core, far], self.tr1[far]).astype(BF16)
        self.copies(1).start()

    def z_start(self):
        s = self.spot
        near = tile_sum(self.tsend[s.core, s.xl], self.tr1[s.xl])
        self.copies(1).wait_recv()
        self.rows[...] = (near + self.tr2[...].astype(F32)).reshape(self.plan.tt * 16, 128)
        self.z_send_rows()

    def pair_back(self):
        s = self.spot
        self.z_take_rows()
        self.wall[s.core, s.xl] = self.rows[...].astype(BF16).reshape(self.plan.tt, 16, 128)
        self.copies(2).start()
        self.copies(3).start()

    def hand_over(self):
        self.copies(2).wait_recv()
        self.copies(4).start()

    def finish(self):
        self.copies(3).wait_recv()
        self.copies(4).wait_recv()

    def drain(self):
        for n in range(5):
            self.copies(n).wait_send()
        self.z_drain()


def normed_of(v):
    centred = v - jnp.mean(v, axis=-1, keepdims=True)
    inv = lax.rsqrt(jnp.mean(centred * centred, axis=-1, keepdims=True) + NORM_EPS)
    return centred * inv, inv


def norm_back(up, normed, inv):
    return inv * (
        up
        - jnp.mean(up, axis=-1, keepdims=True)
        - normed * jnp.mean(up * normed, axis=-1, keepdims=True)
    )


FAR = (
    "w_qkv", "w_proj", "w_up", "w_downt", "order", "back",
    "even_lane", "odd_lane", "tsum", "ccol",
)
LANES = ("even_lane", "odd_lane")
QUARTERS = (4, QUARTER + EXTRA, PACK)
SCRATCH = dict(
    packed=(QUARTERS, F32),
    outward=(QUARTERS, BF16),
    frame=(QUARTERS, BF16),
    tn=((TLANES, TROWS, 128), F32),
    lined=((2, TROWS, KCOLS), F32),
    spread=((2 * TROWS, KCOLS), F32),
    bars=((2, WIN, WIN), F32),
    xs=((CELLS, C), F32),
    gm=((CELLS, C), BF16),
    act=((CELLS, C), BF16),
    q=((CELLS, C), BF16),
    k=((CELLS, C), BF16),
    v=((CELLS, C), BF16),
    qkvt=((NWIN, 3 * C, WIN), BF16),
    ot=((NWIN, C, WIN), BF16),
    dot=((NWIN, C, WIN), BF16),
    dh=((CELLS, C), BF16),
    dout=((CELLS, C), BF16),
    b=((CELLS, C), BF16),
    m=((CELLS, MLP), BF16),
    du=((CELLS, MLP), BF16),
    dqkvt=((3 * C, WIN), BF16),
    back=((CELLS, C), F32),
    wqkvt=((3 * C, C), BF16),
    bias=((NWIN * HEADS, WIN, WIN), F32),
    prob=((NWIN * HEADS, WIN, WIN), F32),
    probb=((NWIN * HEADS, WIN, WIN), BF16),
    dcol=((PAIRS, 2 * TROWS, WIN), F32),
    early=((C, ECOLS), F32),
    late=((C, LCOLS), F32),
    lsum=((3 * C, C), F32),
    tgrad=((TROWS, TLANES * 128), F32),
    send=((4, QUARTER, C), BF16),
    hrecv=((4, QUARTER, C), BF16),
)


def block_kernel(plan, sums, *refs):
    x_ref, g_ref, valid_ref, slab_ref, table_ref = refs[:5]
    far = refs[5 : 5 + len(FAR)]
    refs = refs[5 + len(FAR) :]
    home_ref, early_ref, late_ref, tall_ref = refs[:4]
    near = dict(zip(FAR, refs[4 : 4 + len(FAR)]))
    refs = refs[4 + len(FAR) :]
    s = dict(zip(SCRATCH, refs))
    refs = refs[len(SCRATCH) :]
    fs, es, er, hs, hr, outs = refs[:6]
    refs = refs[6:]
    spot = Spot(plan)
    early, late, table = sums
    for one in sums:
        one.bind(spot, refs[: len(one.names)])
        refs = refs[len(one.names) :]
    before, after = neighbours(plan)
    for place in before + after:
        greet(place)
    greeted = spot.greet_all() + 6
    fetch = [pltpu.make_async_copy(src, near[name], fs.at[n]) for n, (name, src) in enumerate(zip(FAR, far))]
    for copy in fetch:
        copy.start()
    w_qkv, w_proj, w_up, w_downt, order_ref, back_ref, tsum_ref, ccol_ref = (
        near[n] for n in ("w_qkv", "w_proj", "w_up", "w_downt", "order", "back", "tsum", "ccol")
    )

    hm = []
    lane = lax.broadcasted_iota(jnp.int32, (1, C), 1)
    for h in range(HEADS):
        hm.append(jnp.where(lane // HEAD_DIM == h, 1.0, 0.0).astype(BF16))
    scale = HEAD_DIM ** (-0.5)

    slab = slab_ref[...]
    packed, outward, frame = s["packed"], s["outward"], s["frame"]
    packed[:, QUARTER:, :] = jnp.zeros((4, EXTRA, PACK), F32)
    for part, ref in enumerate((x_ref, g_ref)):
        rows = dot(slab, ref[...])
        for c in range(WW):
            for rs in range(2):
                piece = rows[rs * SLAB : (rs + 1) * SLAB, c * C : (c + 1) * C]
                if part == 1:
                    piece = piece * valid_ref[0, c].astype(F32)
                packed[
                    rs * 2 + c // CH, (c % CH) * SLAB : (c % CH + 1) * SLAB, part * C : (part + 1) * C
                ] = piece
    for c in range(WW):
        mark = jnp.full((1, PACK), valid_ref[0, c].astype(F32), F32)
        for rs in range(2):
            packed[rs * 2 + c // CH, QUARTER + c % CH : QUARTER + c % CH + 1, :] = mark
    outward[...] = packed[...].astype(BF16)
    pl.semaphore_wait(pltpu.get_barrier_semaphore(), greeted)
    enter = []
    for lanes in (pl.ds(0, 2 * 128), pl.ds(2 * 128, 128)):
        for out, into, place in zip((2, 1, 0), (1, 2, 3), before):
            n = len(enter)
            enter.append(
                remote(outward.at[out, :, lanes], frame.at[into, :, lanes], es.at[n], er.at[n], place)
            )
    for copy in enter:
        copy.start()
    frame[0] = outward[3]

    blank = jnp.zeros((NWIN, TLANES * 128 - TCOLS), F32)
    for h in range(HEADS):
        for zi in range(WZ):
            for ri in range(WH):
                pieces = [table_ref[:, at : at + TSEG] for at in segments(h, zi, ri)]
                line = jnp.concatenate(pieces + [blank], axis=1)
                rows = pl.ds(h * ZR + zi * WH + ri, NWIN, stride=HEADS * ZR)
                for l in range(TLANES):
                    s["tn"][l, rows, :] = line[:, l * 128 : (l + 1) * 128]
    for copy in fetch:
        copy.wait()
    left = jnp.concatenate([s["tn"][l] for l in range(TLANES)], axis=1)[:, :TCOLS]
    for n in range(3):
        term = left.astype(BF16)
        left = left - term.astype(F32)
        for odd in range(2):
            part = dot(term, near[LANES[odd]][...])
            if n == 0:
                s["lined"][odd] = part
            else:
                s["lined"][odd] += part
    for i in range(NWIN * HEADS):
        for odd in range(2):
            s["spread"][i * STRIP + odd * ZR : i * STRIP + (odd + 1) * ZR, :] = s["lined"][
                odd, i * ZR : (i + 1) * ZR, :
            ]
    for t in range(NWIN):
        for pair in range(PAIRS):
            first = (WW - 1 - 2 * pair) * ZR
            rows = s["spread"][t * HEADS * STRIP : (t + 1) * HEADS * STRIP, first : first + WIN]
            s["bias"][t * HEADS : (t + 1) * HEADS, pair * STRIP : (pair + 1) * STRIP, :] = rows.reshape(
                HEADS, STRIP, WIN
            )
    s["wqkvt"][...] = w_qkv[...].T
    ccol = ccol_ref[...]
    ii = lax.broadcasted_iota(jnp.int32, (WIN, WIN), 0)
    jj = lax.broadcasted_iota(jnp.int32, (WIN, WIN), 1)
    low_i, low_j = (lax.rem(ii, WH) >= RH).astype(jnp.int32), (lax.rem(jj, WH) >= RH).astype(jnp.int32)
    open_rows = jnp.where(lax.axis_index("lat") == plan.lat - 1, 0, 1)
    top_i, top_j = lax.rem(ii // WH, WZ), lax.rem(jj // WH, WZ)
    s["bars"][0] = jnp.where((low_i == low_j) | (open_rows == 1), 0.0, MASKED)
    s["bars"][1] = jnp.where(top_i == top_j, 0.0, MASKED)
    for copy in enter[:3]:
        copy.wait_recv()

    s["xs"][...] = dot(order_ref[...], frame[:, :QUARTER, : 2 * 128].reshape(CELLS, 2 * 128))[:, :C]

    marks = jnp.concatenate(
        [
            frame[0, QUARTER : QUARTER + EXTRA, :WIN][:CH].astype(F32),
            frame[1, QUARTER : QUARTER + EXTRA, :WIN][:CH].astype(F32),
            jnp.zeros((EXTRA - WW, WIN), F32),
        ],
        axis=0,
    ).astype(BF16)
    same = dot(ccol, marks) == lax.dot_general(
        marks, ccol, (((0,), (1,)), ((), ())), preferred_element_type=F32
    )
    barred = jnp.where(same, s["bars"][0], MASKED)
    s["bars"][0] = barred
    s["bars"][1] = jnp.minimum(barred, s["bars"][1])

    normed, inv = normed_of(s["xs"][...])
    a = normed.astype(BF16)
    s["act"][...] = a
    s["q"][...] = dot(a, w_qkv[:, :C]).astype(BF16)
    s["k"][...] = dot(a, w_qkv[:, C : 2 * C]).astype(BF16)
    s["v"][...] = dot(a, w_qkv[:, 2 * C :]).astype(BF16)

    def forward(w, carry):
        at = pl.ds(pl.multiple_of(w * WIN, WIN), WIN)
        q, k = s["q"][at, :], s["k"][at, :]
        bar = s["bars"][(w == NWIN - 1).astype(jnp.int32)]
        qkvt = dot_nt(s["wqkvt"][...], s["act"][at, :]).astype(BF16)
        s["qkvt"][w] = qkvt
        heads = pl.ds(w * HEADS, HEADS)
        split = jnp.concatenate([q * hm[h] for h in range(HEADS)], axis=0)
        score = dot_nt(split, k).reshape(HEADS, WIN, WIN) * scale + s["bias"][heads] + bar
        e = jnp.exp(score - jnp.max(score, axis=-1, keepdims=True))
        p = e * (1.0 / jnp.sum(e, axis=-1, keepdims=True))
        s["prob"][heads] = p
        pb = p.astype(BF16)
        s["probb"][heads] = pb
        for h in range(HEADS):
            head = 2 * C + h * HEAD_DIM
            s["ot"][w, h * HEAD_DIM : (h + 1) * HEAD_DIM, :] = dot_nt(
                qkvt[head : head + HEAD_DIM, :], pb[h]
            ).astype(BF16)
        return carry

    lax.fori_loop(0, NWIN, forward, 0)

    for copy in enter[3:]:
        copy.wait_recv()
    cells = dot(order_ref[...], frame[:, :QUARTER, 128:].reshape(CELLS, 2 * 128))
    s["gm"][...] = cells[:, C - 128 :].astype(BF16)
    mixed = jnp.concatenate([dot_tn(s["ot"][w], w_proj[...]) for w in range(NWIN)], axis=0)
    mid = (s["xs"][...] + mixed).astype(BF16).astype(F32)
    n2, inv2 = normed_of(mid)
    b = n2.astype(BF16)
    s["b"][...] = b
    u = dot(b, w_up[...])
    cdf = 0.5 * (1.0 + lax.erf(u * 0.7071067811865476))
    s["m"][...] = (u * cdf).astype(BF16)
    slope = cdf + u * jnp.exp(-0.5 * u * u) * 0.3989422804014327
    g = s["gm"][...]
    du = (dot(g, w_downt[...]) * slope).astype(BF16)
    s["du"][...] = du
    dh = (g.astype(F32) + norm_back(dot_nt(du, w_up[...]), n2, inv2)).astype(BF16)
    s["dh"][...] = dh
    s["dout"][...] = dot_nt(dh, w_proj[...]).astype(BF16)
    for w in range(NWIN):
        s["dot"][w] = dot_nt(w_proj[...], dh[w * WIN : (w + 1) * WIN, :]).astype(BF16)
    s["early"][:, :MLP] = dot_tn(s["b"][...], s["du"][...])
    s["early"][:, MLP:] = dot_tn(s["gm"][...], s["m"][:, :DOWN])
    early.fill(s["early"])
    early.core_start()

    for w in range(NWIN):
        at = pl.ds(w * WIN, WIN)
        k, v, do = s["k"][at, :], s["v"][at, :], s["dout"][at, :]
        split = jnp.concatenate([do * hm[h] for h in range(HEADS)], axis=0)
        dp = dot_nt(split, v).reshape(HEADS, WIN, WIN)
        p = s["prob"][w * HEADS : (w + 1) * HEADS]
        ds = p * (dp - jnp.sum(p * dp, axis=-1, keepdims=True))
        dsb = ds.astype(BF16)
        for h in range(HEADS):
            first = (w * HEADS + h) * STRIP
            for pair in range(PAIRS):
                s["dcol"][pair, first : first + STRIP, :] = ds[h, pair * STRIP : (pair + 1) * STRIP, :]
            low, high = h * HEAD_DIM, (h + 1) * HEAD_DIM
            kt, qt = s["qkvt"][w, C + low : C + high, :], s["qkvt"][w, low:high, :]
            s["dqkvt"][low:high, :] = (dot_nt(kt, dsb[h]) * scale).astype(BF16)
            s["dqkvt"][C + low : C + high, :] = (dot(qt, dsb[h]) * scale).astype(BF16)
            s["dqkvt"][2 * C + low : 2 * C + high, :] = dot(
                s["dot"][w, low:high, :], s["probb"][w * HEADS + h]
            ).astype(BF16)
        dqkvt = s["dqkvt"][...]
        s["back"][at, :] = dot(w_qkv[...], dqkvt).T
        term = dot(dqkvt, s["act"][at, :])
        if w == 0:
            s["lsum"][...] = term
        else:
            s["lsum"][...] += term
        if w == NWIN - 2:
            early.plane_start()

    grad = jnp.zeros((2 * TROWS, KCOLS), F32)
    for pair in range(PAIRS):
        grad += dot(s["dcol"][pair].astype(BF16), tsum_ref[pair])
    s["spread"][...] = grad
    for i in range(NWIN * HEADS):
        for odd in range(2):
            s["lined"][odd, i * ZR : (i + 1) * ZR, :] = s["spread"][
                i * STRIP + odd * ZR : i * STRIP + (odd + 1) * ZR, :
            ]
    s["tgrad"][:, TCOLS:] = jnp.zeros((TROWS, TLANES * 128 - TCOLS), F32)
    s["tgrad"][:, :TCOLS] = dot_nt(s["lined"][0].astype(BF16), near["even_lane"][...]) + dot_nt(
        s["lined"][1].astype(BF16), near["odd_lane"][...]
    )
    table.fill(s["tgrad"])
    table.core_start()
    s["late"][:, : 3 * C] = s["lsum"][...].T
    proj = jnp.zeros((C, C), F32)
    for w in range(NWIN):
        proj += dot(s["ot"][w], s["dh"][w * WIN : (w + 1) * WIN, :])
    s["late"][:, 3 * C : 4 * C] = proj
    s["late"][:, 4 * C :] = dot_tn(s["gm"][...], s["m"][:, DOWN:])
    late.fill(s["late"])
    late.core_start()

    normed, inv = normed_of(s["xs"][...])
    dxs = (s["dh"][...].astype(F32) + norm_back(s["back"][...], normed, inv)).astype(BF16)
    s["send"][...] = dot(back_ref[...], dxs).astype(BF16).reshape(4, QUARTER, C)
    home = [
        remote(s["send"].at[1], s["hrecv"].at[2], hs.at[0], hr.at[0], after[0]),
        remote(s["send"].at[2], s["hrecv"].at[1], hs.at[1], hr.at[1], after[1]),
        remote(s["send"].at[3], s["hrecv"].at[0], hs.at[2], hr.at[2], after[2]),
    ]
    table.pair_start()
    late.plane_start()
    for copy in home:
        copy.start()
    home_ref[3] = s["send"][0]

    early.z_start()
    table.z_start()
    late.z_start()
    early.z_back()
    table.z_back()
    late.z_back()
    early.plane_back()
    table.pair_back()
    late.plane_back()
    table.hand_over()
    for copy in home:
        copy.wait_recv()
    for q in range(3):
        home_ref[q] = s["hrecv"][q]
    early.hand_over()
    late.hand_over()
    leave = []
    for n, (one, out) in enumerate(((table, tall_ref), (early, early_ref), (late, late_ref))):
        one.finish()
        leave.append(pltpu.make_async_copy(one.wall, out, outs.at[n]))
        leave[-1].start()
    for copy in enter + home:
        copy.wait_send()
    for one in sums:
        one.drain()
    for copy in leave:
        copy.wait()


def block(plan, state, cotangent, valid, table, w_qkv, w_proj, w_up, w_down):
    vmem = pl.BlockSpec(memory_space=pltpu.VMEM)
    hbm = pl.BlockSpec(memory_space=pl.ANY)
    order = cell_order()
    sums = (WeightSum(plan, ECOLS, False), WeightSum(plan, LCOLS, False), TableSum(plan))
    consts = (
        order, order.T, table_lanes(0), table_lanes(1), table_sums(), column_of_cell(),
    )
    far = [w_qkv, w_proj, w_up, w_down.T] + [jnp.asarray(m, BF16) for m in consts]
    scratch = [pltpu.VMEM(v.shape, v.dtype) for v in far]
    scratch += [pltpu.VMEM(shape, dtype) for shape, dtype in SCRATCH.values()]
    sem = pltpu.SemaphoreType.DMA
    scratch += [sem((len(FAR),)), sem((6,)), sem((6,)), sem((3,)), sem((3,)), sem((3,))]
    for one in sums:
        scratch += one.scratch()
    rows = lambda v: v.transpose(1, 0, 2).reshape(WH * LEVELS, WW * C)
    return pl.pallas_call(
        functools.partial(block_kernel, plan, sums),
        out_shape=[jax.ShapeDtypeStruct((4, QUARTER, C), BF16)] + [one.out_shape() for one in sums],
        in_specs=[vmem, vmem, pl.BlockSpec(memory_space=pltpu.SMEM), vmem, vmem] + [hbm] * len(far),
        out_specs=[vmem, hbm, hbm, hbm],
        scratch_shapes=scratch,
        compiler_params=pltpu.CompilerParams(
            collective_id=0, has_side_effects=True, vmem_limit_bytes=VMEM_LIMIT
        ),
        name="block",
    )(
        rows(state), rows(cotangent), valid.reshape(1, WW), jnp.asarray(slab_order(), BF16), table, *far
    )


def write_kernel(
    plan, factor, home_ref, early_ref, late_ref, tall_ref, slab_ref,
    dx_ref, qkv_ref, proj_ref, up_ref, down_ref, table_ref, band, early, late, tgrad,
):
    jobs = (
        (early_ref, early, ECOLS // 128, C // 16, plan.plane, factor),
        (late_ref, late, LCOLS // 128, C // 16, plan.plane, factor),
        (tall_ref, tgrad, TLANES, TROWS // 16, XL, 1.0),
    )
    for src, dst, lanes, rows, parts, gain in jobs:
        tiles = src.shape[2]
        for i in range(rows * lanes):
            core, rest = divmod(i, parts * tiles)
            r, l = divmod(i, lanes)
            value = src[core, rest // tiles, rest % tiles].astype(F32)
            if dst is tgrad:
                dst[l, r * 16 : r * 16 + 16, :] = value
            else:
                dst[r * 16 : r * 16 + 16, l * 128 : l * 128 + 128] = value * gain
    up_ref[...] = early[:, :MLP]
    down_ref[:, :DOWN] = early[:, MLP:]
    down_ref[:, DOWN:] = late[:, 4 * C :]
    proj_ref[...] = late[:, 3 * C : 4 * C]
    qkv_ref[...] = late[:, : 3 * C]
    for h in range(HEADS):
        for zi in range(WZ):
            for ri in range(WH):
                rows = pl.ds(h * ZR + zi * WH + ri, NWIN, stride=HEADS * ZR)
                line = jnp.concatenate(
                    [tgrad[l, rows, :] for l in range(TLANES)], axis=1
                )
                for zj, at in enumerate(segments(h, zi, ri)):
                    table_ref[:, at : at + TSEG] = line[:, zj * TSEG : (zj + 1) * TSEG]
    for c in range(WW):
        for rs in range(2):
            band[rs * SLAB : (rs + 1) * SLAB, c * C : (c + 1) * C] = home_ref[
                rs * 2 + c // CH, (c % CH) * SLAB : (c % CH + 1) * SLAB, :
            ].astype(F32)
    dx_ref[...] = dot(slab_ref[...], band[...].astype(BF16)).astype(BF16)


def write(plan, home, early, late, tall):
    vmem = pl.BlockSpec(memory_space=pltpu.VMEM)
    factor = float(CELLS * plan.lon * plan.lat) ** (-0.5)
    dx, qkv, proj, up, down, table = pl.pallas_call(
        functools.partial(write_kernel, plan, factor),
        out_shape=(
            jax.ShapeDtypeStruct((WH * LEVELS, WW * C), BF16),
            jax.ShapeDtypeStruct((C, 3 * C), F32),
            jax.ShapeDtypeStruct((C, C), F32),
            jax.ShapeDtypeStruct((C, MLP), F32),
            jax.ShapeDtypeStruct((C, MLP), F32),
            jax.ShapeDtypeStruct((NWIN, HEADS * ZR * ZR * SPAN), F32),
        ),
        in_specs=[vmem] * 5,
        out_specs=(vmem,) * 6,
        scratch_shapes=[
            pltpu.VMEM((2 * SLAB, WW * C), F32),
            pltpu.VMEM((C, ECOLS), F32),
            pltpu.VMEM((C, LCOLS), F32),
            pltpu.VMEM((TLANES, TROWS, 128), F32),
        ],
        compiler_params=pltpu.CompilerParams(vmem_limit_bytes=VMEM_LIMIT),
        name="write",
    )(home, early, late, tall, jnp.asarray(slab_order().T, BF16))
    dx = dx.reshape(WH, LEVELS, WW * C).transpose(1, 0, 2)
    return dx, qkv, proj, up, down.T, table


def per_device(plan, state_in, cotangent, w_qkv, w_proj, w_up, w_down, bias_table, pad_valid):
    return write(plan, *block(plan, state_in, cotangent, pad_valid, bias_table, w_qkv, w_proj, w_up, w_down))


def solution(mesh):
    plan = Plan(mesh.shape["lon"], mesh.shape["lat"])
    return jax.shard_map(
        functools.partial(per_device, plan),
        mesh=mesh,
        in_specs=(
            P(None, "lat", "lon"),
            P(None, "lat", "lon"),
            P(),
            P(),
            P(),
            P(),
            P("lat", None),
            P("lon"),
        ),
        out_specs=(P(None, "lat", "lon"), P(), P(), P(), P(), P("lat", None)),
        check_vma=False,
    )
```
